32 devices in a mesh: ctx: 8 (over z, y), head: 4 (over x, core).
Axes of the slice: x: 2, y: 2, z: 4, core: 2. Of those that a mesh axis runs over, the one named last changes fastest.
Arguments:
- queries: bfloat16 [4096, 4096], P('ctx', 'head'), may hold values from -8 to 8
- keys: bfloat16 [4096, 1024], P('ctx', 'head'), may hold values from -8 to 8
- values: bfloat16 [4096, 1024], P('ctx', 'head'), may hold values from -6 to 6
- output_gradient: bfloat16 [4096, 4096], P('ctx', 'head'), may hold values from -6 to 6
- blocks: int32 [32, 8], P('ctx'), may hold values from 0 to 31, as said below
- counts: int32 [32], P('ctx'), may hold values from 2 to 8, as said below
Outputs:
- dqueries: bfloat16 [4096, 4096], P(('ctx', 'head'))
- dkeys: bfloat16 [4096, 1024], P(('ctx', 'head'))
- dvalues: bfloat16 [4096, 1024], P(('ctx', 'head'))
The draws below stay inside these ranges and needn't reach their ends.
Inputs may be any that keep to these rules, and one draw needn't show every extreme that they name: For the query block b on token shard i = b // 4, all 8 entries of row b are distinct and name key blocks of the shards i - 2 to i + 2, taken around the closed cycle of 32 blocks. `counts`: some rows have all 8 entries live.
All inputs are finite; a program needn't handle non-finite values.
Results may differ from the reference program's by a relative error of at most 0.0088.
Values may be sent and summed in bfloat16 or wider, within the bound.
No kernel may reach another device: no remote copies, remote signals or barrier semaphores. Data moves between devices by JAX's collectives and lax.ppermute only.
A program may use at most 64 MiB of HBM per device.

```python
import math
import jax
import jax.numpy as jnp
from jax import lax

HEAD_SIZE = 128
QUERY_HEADS = 32
KEY_VALUE_HEADS = 8
BLOCK_TOKENS = 128
SLOTS = 8
REACH = 2
ARRAY_TOKENS = 4096
QB_DEV = 4
QUERY_BLOCKS = 32


def draw_queries(key, part):
    final_gradients = jnp.clip(jax.random.normal(jax.random.fold_in(key, 19), (ARRAY_TOKENS, QUERY_HEADS, HEAD_SIZE), jnp.float32), -6.0, 6.0)
    return final_gradients.reshape(ARRAY_TOKENS, QUERY_HEADS * HEAD_SIZE).astype(jnp.bfloat16)


def draw_keys(key, part):
    final_gradients = jnp.clip(jax.random.normal(jax.random.fold_in(key, 29), (ARRAY_TOKENS, KEY_VALUE_HEADS, HEAD_SIZE), jnp.float32), -6.0, 6.0)
    return final_gradients.reshape(ARRAY_TOKENS, KEY_VALUE_HEADS * HEAD_SIZE).astype(jnp.bfloat16)


def draw_blocks(key, part):
    window_size = (2 * REACH + 1) * QB_DEV
    subkeys = jax.random.split(jax.random.fold_in(key, 11), QUERY_BLOCKS)

    def pick_slots(subkey):
        return jax.random.permutation(subkey, window_size)[:SLOTS]
    chosen = jax.vmap(pick_slots)(subkeys).astype(jnp.int32)
    positions = jnp.arange(QUERY_BLOCKS, dtype=jnp.int32)
    window_start = (positions // QB_DEV - REACH) * QB_DEV
    return jnp.mod(window_start[:, None] + chosen, QUERY_BLOCKS).astype(jnp.int32)


def draw_counts(key, part):
    drawn = jax.random.randint(jax.random.fold_in(key, 13), (QUERY_BLOCKS,), 2, SLOTS + 1)
    positions = jnp.arange(QUERY_BLOCKS, dtype=jnp.int32)
    drawn = jnp.where(positions % 5 == 0, SLOTS, drawn)
    drawn = jnp.where(positions % 7 == 3, 2, drawn)
    return drawn.astype(jnp.int32)


def block_levels(stream_key, dims, cuts, least, high):
    gain, own = 1.0, jax.random.fold_in(stream_key, 6)
    for dim, parts in cuts:
        draws = jnp.exp(jax.random.uniform(jax.random.fold_in(own, dim), (parts,), jnp.float32, least / len(cuts), high / len(cuts)))
        gain = gain * jnp.repeat(draws, dims[dim] // parts).reshape([-1 if axis == dim else 1 for axis in range(len(dims))])
    return gain


def bell_draw(stream_key, dims, width, most, pieces=(), held_as=jnp.bfloat16):
    values = jax.random.normal(stream_key, dims, jnp.float32) * width
    if len(pieces) > 0:
        values = block_levels(stream_key, dims, pieces, -0.22, 0.18) * values
    return jnp.clip(values, min=-most, max=most).astype(held_as)


def setup_inputs(seed: int = 0) -> dict:
    key_of = jax.random.split(jax.random.key(seed), 7)
    return {
        "queries": draw_queries(jax.random.fold_in(key_of[6], 71), 0),
        "keys": draw_keys(jax.random.fold_in(key_of[6], 71), 0),
        "values": bell_draw(key_of[2], (ARRAY_TOKENS, KEY_VALUE_HEADS * HEAD_SIZE), 1.0, 6.0, ((0, 8), (1, 4))),
        "output_gradient": bell_draw(key_of[3], (ARRAY_TOKENS, QUERY_HEADS * HEAD_SIZE), 1.0, 6.0, ((0, 8), (1, 4))),
        "blocks": draw_blocks(jax.random.fold_in(key_of[6], 71), 0),
        "counts": draw_counts(jax.random.fold_in(key_of[6], 71), 0),
    }


def reference(queries, keys, values, output_gradient, blocks, counts):
    query_group = QUERY_HEADS // KEY_VALUE_HEADS
    softmax_scale = 1.0 / math.sqrt(HEAD_SIZE)
    blocked_queries = queries.reshape(QUERY_BLOCKS, BLOCK_TOKENS, KEY_VALUE_HEADS, query_group, HEAD_SIZE)
    output_blocks = output_gradient.reshape(QUERY_BLOCKS, BLOCK_TOKENS, KEY_VALUE_HEADS, query_group, HEAD_SIZE)
    blocked_keys = keys.reshape(QUERY_BLOCKS, BLOCK_TOKENS, KEY_VALUE_HEADS, HEAD_SIZE)
    blocked_values = values.reshape(QUERY_BLOCKS, BLOCK_TOKENS, KEY_VALUE_HEADS, HEAD_SIZE)

    def qblock_step(running, qblock):
        key_gradient_sum, value_gradient_sum = running
        slot_blocks = blocks[qblock]
        live_slots = jnp.arange(SLOTS) < counts[qblock]
        live_mask = live_slots[None, None, None, :, None]
        kblock = blocked_keys[slot_blocks].astype(jnp.float32)
        vblock = blocked_values[slot_blocks].astype(jnp.float32)
        qrows = blocked_queries[qblock].astype(jnp.float32)
        orows = output_blocks[qblock].astype(jnp.float32)
        scores = jnp.einsum('rhgd,schd->hgrsc', qrows, kblock) * softmax_scale
        scores = jnp.where(live_mask, scores, -1e+30)
        row_max = lax.optimization_barrier(jnp.max(scores, axis=(3, 4), keepdims=True))
        weights = jnp.where(live_mask, jnp.exp(scores - row_max), 0.0)
        probs = weights / lax.optimization_barrier(jnp.sum(weights, axis=(3, 4), keepdims=True))
        dprobs = jnp.einsum('rhgd,schd->hgrsc', orows, vblock)
        row_delta = lax.optimization_barrier(jnp.sum(probs * dprobs, axis=(3, 4), keepdims=True))
        dscores = lax.optimization_barrier((probs * (dprobs - row_delta)).astype(jnp.bfloat16)).astype(jnp.float32)
        probs_bf = lax.optimization_barrier(probs.astype(jnp.bfloat16)).astype(jnp.float32)
        dquery = softmax_scale * jnp.einsum('hgrsc,schd->rhgd', dscores, kblock)
        dkey_part = softmax_scale * jnp.einsum('hgrsc,rhgd->schd', dscores, qrows)
        dvalue_part = jnp.einsum('hgrsc,rhgd->schd', probs_bf, orows)
        key_gradient_sum = key_gradient_sum.at[slot_blocks].add(dkey_part)
        value_gradient_sum = value_gradient_sum.at[slot_blocks].add(dvalue_part)
        return ((key_gradient_sum, value_gradient_sum), dquery.astype(jnp.bfloat16).reshape(BLOCK_TOKENS, QUERY_HEADS * HEAD_SIZE))
    empty_gradient = jnp.zeros((QUERY_BLOCKS, BLOCK_TOKENS, KEY_VALUE_HEADS, HEAD_SIZE), jnp.float32)
    (key_gradient_sum, value_gradient_sum), dquery_rows = lax.scan(qblock_step, (empty_gradient, empty_gradient), jnp.arange(QUERY_BLOCKS, dtype=jnp.int32))
    dqueries = dquery_rows.reshape(ARRAY_TOKENS, QUERY_HEADS * HEAD_SIZE)
    dkeys = key_gradient_sum.reshape(ARRAY_TOKENS, KEY_VALUE_HEADS * HEAD_SIZE).astype(jnp.bfloat16)
    dvalues = value_gradient_sum.reshape(ARRAY_TOKENS, KEY_VALUE_HEADS * HEAD_SIZE).astype(jnp.bfloat16)
    return (dqueries, dkeys, dvalues)
```

```python
import functools
import math

import jax
import jax.numpy as jnp
from jax import lax
from jax.experimental import pallas as pl
from jax.experimental.pallas import tpu as pltpu
from jax.sharding import PartitionSpec as P

HEAD_SIZE = 128
BLOCK_TOKENS = 128
SLOTS = 8
REACH = 2
SHARDS = 2 * REACH + 1
F32 = jnp.float32
BF16 = jnp.bfloat16
ROWS_BY_ROWS = (((1,), (1,)), ((), ()))
COLS_BY_COLS = (((0,), (0,)), ((), ()))


def attention_kernel(
    cycle_blocks, blocks_ref, counts_ref, me_ref, queries_hbm, outgrad_hbm, *refs
):
    window_hbm = refs[:SHARDS]
    dqueries_ref = refs[SHARDS]
    partial_refs = refs[SHARDS + 1 : 2 * SHARDS + 1]
    (
        queries,
        outgrad,
        window,
        sums,
        scores_ref,
        dprobs_ref,
        probs_ref,
        block_keys,
        block_values,
        sems,
    ) = refs[2 * SHARDS + 1 :]
    tokens, query_width = queries.shape
    kv_width = window.shape[2]
    kv_heads, group = kv_width // HEAD_SIZE, query_width // kv_width
    own_blocks, rows = tokens // BLOCK_TOKENS, group * BLOCK_TOKENS
    scale = 1.0 / math.sqrt(HEAD_SIZE)
    scale_log2 = scale * math.log2(math.e)

    copies = [
        pltpu.make_async_copy(queries_hbm, queries, sems.at[0]),
        pltpu.make_async_copy(outgrad_hbm, outgrad, sems.at[1]),
    ]
    for j in range(SHARDS):
        place = window.at[:, pl.ds(j * tokens, tokens), :]
        copies.append(pltpu.make_async_copy(window_hbm[j], place, sems.at[2 + j]))
    for copy in copies:
        copy.start()
    sums[...] = jnp.zeros_like(sums)
    for copy in copies:
        copy.wait()
    first_block = (me_ref[0] - REACH) * own_blocks

    def head_block(qblock, head, live):
        row_ds = pl.ds(pl.multiple_of(qblock * BLOCK_TOKENS, BLOCK_TOKENS), BLOCK_TOKENS)
        kv_cols = slice(head * HEAD_SIZE, (head + 1) * HEAD_SIZE)
        q_cols = [
            slice((head * group + g) * HEAD_SIZE, (head * group + g + 1) * HEAD_SIZE)
            for g in range(group)
        ]
        slots = [slice(s * BLOCK_TOKENS, (s + 1) * BLOCK_TOKENS) for s in range(live)]
        places = []
        for s in range(live):
            place = lax.rem(blocks_ref[qblock, s] - first_block + cycle_blocks, cycle_blocks)
            place = pl.ds(pl.multiple_of(place * BLOCK_TOKENS, BLOCK_TOKENS), BLOCK_TOKENS)
            places.append(place)
            block_keys[slots[s]] = window[0, place, kv_cols]
            block_values[slots[s]] = window[1, place, kv_cols]
        q = jnp.concatenate([queries[row_ds, c] for c in q_cols], axis=0)
        o = jnp.concatenate([outgrad[row_ds, c] for c in q_cols], axis=0)

        def fold(x, op):
            return op(x.reshape(BLOCK_TOKENS // 8, 8, rows), axis=0)

        top = None
        for s in range(live):
            scores = lax.dot_general(
                block_keys[slots[s]], q, ROWS_BY_ROWS, preferred_element_type=F32
            )
            scores_ref[slots[s]] = scores
            part = fold(scores, jnp.max)
            top = part if s == 0 else jnp.maximum(top, part)
        row_max = jnp.max(top, axis=0, keepdims=True) * scale_log2
        total = weighted = None
        for s in range(live):
            dprobs = lax.dot_general(
                block_values[slots[s]], o, ROWS_BY_ROWS, preferred_element_type=F32
            )
            weights = jnp.exp2(scores_ref[slots[s]] * scale_log2 - row_max)
            dprobs_ref[slots[s]] = dprobs
            probs_ref[slots[s]] = weights.astype(BF16)
            part, wpart = fold(weights, jnp.sum), fold(weights * dprobs, jnp.sum)
            total = part if s == 0 else total + part
            weighted = wpart if s == 0 else weighted + wpart
        inverse = 1.0 / jnp.sum(total, axis=0, keepdims=True)
        row_delta = jnp.sum(weighted, axis=0, keepdims=True) * inverse
        inverse_col = jnp.transpose(jnp.broadcast_to(inverse, (8, rows)))[:, :1]
        q_scaled = (q.astype(F32) * inverse_col).astype(BF16)
        o_scaled = (o.astype(F32) * inverse_col).astype(BF16)
        dq = None
        for s in range(live):
            weights = probs_ref[slots[s]]
            dscores = (weights.astype(F32) * (dprobs_ref[slots[s]] - row_delta)).astype(BF16)
            sums[0, places[s], kv_cols] += jnp.dot(
                dscores, q_scaled, preferred_element_type=F32
            )
            sums[1, places[s], kv_cols] += jnp.dot(
                weights, o_scaled, preferred_element_type=F32
            )
            part = lax.dot_general(
                block_keys[slots[s]], dscores, COLS_BY_COLS, preferred_element_type=F32
            )
            dq = part if s == 0 else dq + part
        dq = jnp.transpose(dq * (inverse * scale)).astype(BF16)
        for g in range(group):
            dqueries_ref[row_ds, q_cols[g]] = dq[g * BLOCK_TOKENS : (g + 1) * BLOCK_TOKENS]

    def one_block(qblock, carry):
        for head in range(kv_heads):
            for live in range(1, SLOTS + 1):
                pl.when(counts_ref[qblock] == live)(
                    functools.partial(head_block, qblock, head, live)
                )
        return carry

    lax.fori_loop(0, own_blocks, one_block, 0)
    for j in range(SHARDS):
        span = slice(j * tokens, (j + 1) * tokens)
        partial_refs[j][0] = (sums[0, span] * scale).astype(BF16)
        partial_refs[j][1] = sums[1, span].astype(BF16)


def attention(cycle_blocks, blocks, counts, me, queries, output_gradient, window):
    tokens, query_width = queries.shape
    kv_width = window[0].shape[2]
    rows = query_width // kv_width * BLOCK_TOKENS
    vmem = pl.BlockSpec(memory_space=pltpu.VMEM)
    smem = pl.BlockSpec(memory_space=pltpu.SMEM)
    hbm = pl.BlockSpec(memory_space=pl.ANY)
    return pl.pallas_call(
        functools.partial(attention_kernel, cycle_blocks),
        out_shape=[jax.ShapeDtypeStruct(queries.shape, BF16)]
        + [jax.ShapeDtypeStruct(piece.shape, BF16) for piece in window],
        in_specs=[smem] * 3 + [hbm] * (2 + SHARDS),
        out_specs=[vmem] * (1 + SHARDS),
        scratch_shapes=[
            pltpu.VMEM(queries.shape, BF16),
            pltpu.VMEM(queries.shape, BF16),
            pltpu.VMEM((2, SHARDS * tokens, kv_width), BF16),
            pltpu.VMEM((2, SHARDS * tokens, kv_width), F32),
            pltpu.VMEM((SLOTS * BLOCK_TOKENS, rows), F32),
            pltpu.VMEM((SLOTS * BLOCK_TOKENS, rows), F32),
            pltpu.VMEM((SLOTS * BLOCK_TOKENS, rows), BF16),
            pltpu.VMEM((SLOTS * BLOCK_TOKENS, HEAD_SIZE), BF16),
            pltpu.VMEM((SLOTS * BLOCK_TOKENS, HEAD_SIZE), BF16),
            pltpu.SemaphoreType.DMA((2 + SHARDS,)),
        ],
        compiler_params=pltpu.CompilerParams(vmem_limit_bytes=40 * 2**20),
        cost_estimate=pl.CostEstimate(
            flops=5 * 10**9, bytes_accessed=10**7, transcendentals=4 * 10**6
        ),
    )(blocks, counts, me, queries, output_gradient, *window)


def from_behind(x, by):
    size = lax.axis_size("ctx")
    return lax.ppermute(x, "ctx", [(i, (i + by) % size) for i in range(size)])


def on_device(queries, keys, values, output_gradient, blocks, counts):
    tokens = queries.shape[0]
    cycle_blocks = lax.axis_size("ctx") * (tokens // BLOCK_TOKENS)
    me = lax.axis_index("ctx").reshape(1)
    stacked = jnp.stack([keys, values])
    offsets = range(-REACH, REACH + 1)
    window = [stacked if o == 0 else from_behind(stacked, -o) for o in offsets]
    dqueries, *partials = attention(
        cycle_blocks, blocks, counts, me, queries, output_gradient, window
    )
    summed = partials[REACH].astype(F32)
    for offset, piece in zip(offsets, partials):
        if offset != 0:
            summed = summed + from_behind(piece, offset).astype(F32)
    summed = summed.astype(BF16)

    def exchange(x):
        return lax.all_to_all(x, "head", split_axis=0, concat_axis=1, tiled=True)

    return exchange(dqueries), exchange(summed[0]), exchange(summed[1])


def solution(mesh):
    return jax.shard_map(
        on_device,
        mesh=mesh,
        in_specs=(
            P("ctx", "head"),
            P("ctx", "head"),
            P("ctx", "head"),
            P("ctx", "head"),
            P("ctx", None),
            P("ctx"),
        ),
        out_specs=(P(("ctx", "head"), None), P(("ctx", "head"), None), P(("ctx", "head"), None)),
        check_vma=False,
    )
```

```python
import functools
import math

import jax
import jax.numpy as jnp
from jax import lax
from jax.experimental import pallas as pl
from jax.experimental.pallas import tpu as pltpu
from jax.sharding import PartitionSpec as P

HEAD_SIZE = 128
BLOCK_TOKENS = 128
SLOTS = 8
REACH = 2
SHARDS = 2 * REACH + 1
F32 = jnp.float32
BF16 = jnp.bfloat16
ROWS_BY_ROWS = (((1,), (1,)), ((), ()))
COLS_BY_COLS = (((0,), (0,)), ((), ()))


def attention_kernel(
    head, cycle_blocks, places_out, blocks_ref, counts_ref, me_ref, queries_hbm, outgrad_hbm, *refs
):
    window_hbm = refs[:SHARDS]
    dqueries_refs = refs[SHARDS : SHARDS + places_out]
    partial_refs = refs[SHARDS + places_out : 2 * SHARDS + places_out]
    (
        dqueries_ref,
        queries,
        outgrad,
        window,
        sums,
        scores_ref,
        dprobs_ref,
        block_keys,
        block_values,
        sems,
    ) = refs[2 * SHARDS + places_out :]
    tokens, query_width = queries.shape
    group = query_width // HEAD_SIZE
    own_blocks, rows = tokens // BLOCK_TOKENS, group * BLOCK_TOKENS
    scale = 1.0 / math.sqrt(HEAD_SIZE)
    scale_log2 = scale * math.log2(math.e)

    columns = pl.ds(head * query_width, query_width)
    copies = [
        pltpu.make_async_copy(queries_hbm.at[:, columns], queries, sems.at[0]),
        pltpu.make_async_copy(outgrad_hbm.at[:, columns], outgrad, sems.at[1]),
    ]
    for j in range(SHARDS):
        place = window.at[:, pl.ds(j * tokens, tokens), :]
        copies.append(pltpu.make_async_copy(window_hbm[j], place, sems.at[2 + j]))
    for copy in copies:
        copy.start()
    sums[...] = jnp.zeros_like(sums)
    for copy in copies:
        copy.wait()
    first_block = (me_ref[0] - REACH) * own_blocks

    def query_block(qblock, live):
        row_ds = pl.ds(pl.multiple_of(qblock * BLOCK_TOKENS, BLOCK_TOKENS), BLOCK_TOKENS)
        q_cols = [slice(g * HEAD_SIZE, (g + 1) * HEAD_SIZE) for g in range(group)]
        slots = [slice(s * BLOCK_TOKENS, (s + 1) * BLOCK_TOKENS) for s in range(live)]
        places = []
        for s in range(live):
            place = lax.rem(blocks_ref[qblock, s] - first_block + cycle_blocks, cycle_blocks)
            place = pl.ds(pl.multiple_of(place * BLOCK_TOKENS, BLOCK_TOKENS), BLOCK_TOKENS)
            places.append(place)
            block_keys[slots[s]] = window[0, place]
            block_values[slots[s]] = window[1, place]
        q = jnp.concatenate([queries[row_ds, c] for c in q_cols], axis=0)
        o = jnp.concatenate([outgrad[row_ds, c] for c in q_cols], axis=0)

        def fold(x, op):
            return op(x.reshape(BLOCK_TOKENS // 8, 8, rows), axis=0)

        top = None
        for s in range(live):
            scores = lax.dot_general(
                block_keys[slots[s]], q, ROWS_BY_ROWS, preferred_element_type=F32
            )
            scores_ref[slots[s]] = scores
            part = fold(scores, jnp.max)
            top = part if s == 0 else jnp.maximum(top, part)
        row_max = jnp.max(top, axis=0, keepdims=True) * scale_log2
        total = weighted = None
        for s in range(live):
            dprobs = lax.dot_general(
                block_values[slots[s]], o, ROWS_BY_ROWS, preferred_element_type=F32
            )
            weights = jnp.exp2(scores_ref[slots[s]] * scale_log2 - row_max)
            dprobs_ref[slots[s]] = dprobs
            scores_ref[slots[s]] = weights
            part, wpart = fold(weights, jnp.sum), fold(weights * dprobs, jnp.sum)
            total = part if s == 0 else total + part
            weighted = wpart if s == 0 else weighted + wpart
        inverse = 1.0 / jnp.sum(total, axis=0, keepdims=True)
        row_delta = jnp.sum(weighted, axis=0, keepdims=True) * inverse
        dq = None
        for s in range(live):
            probs = scores_ref[slots[s]] * inverse
            dscores = (probs * (dprobs_ref[slots[s]] - row_delta)).astype(BF16)
            sums[0, places[s]] += jnp.dot(dscores, q, preferred_element_type=F32)
            sums[1, places[s]] += jnp.dot(
                probs.astype(BF16), o, preferred_element_type=F32
            )
            part = lax.dot_general(
                block_keys[slots[s]], dscores, COLS_BY_COLS, preferred_element_type=F32
            )
            dq = part if s == 0 else dq + part
        dq = jnp.transpose(dq * scale).astype(BF16)
        for g in range(group):
            dqueries_ref[row_ds, q_cols[g]] = dq[g * BLOCK_TOKENS : (g + 1) * BLOCK_TOKENS]

    def one_block(qblock, carry):
        for live in range(1, SLOTS + 1):
            pl.when(counts_ref[qblock] == live)(functools.partial(query_block, qblock, live))
        return carry

    lax.fori_loop(0, own_blocks, one_block, 0)
    share = tokens // places_out
    for k in range(places_out):
        first = pl.multiple_of((me_ref[1] ^ k) * share, share)
        dqueries_refs[k][...] = dqueries_ref[pl.ds(first, share)]
    for j in range(SHARDS):
        span = slice(j * tokens, (j + 1) * tokens)
        partial_refs[j][0] = (sums[0, span] * scale).astype(BF16)
        partial_refs[j][1] = sums[1, span].astype(BF16)


def attention(head, heads, cycle_blocks, places_out, blocks, counts, me, queries, output_gradient, window):
    tokens, query_width = queries.shape
    query_width //= heads
    kv_width = window[0].shape[2]
    rows = query_width // kv_width * BLOCK_TOKENS
    vmem = pl.BlockSpec(memory_space=pltpu.VMEM)
    smem = pl.BlockSpec(memory_space=pltpu.SMEM)
    hbm = pl.BlockSpec(memory_space=pl.ANY)
    return pl.pallas_call(
        functools.partial(attention_kernel, head, cycle_blocks, places_out),
        out_shape=[jax.ShapeDtypeStruct((tokens // places_out, query_width), BF16)] * places_out
        + [jax.ShapeDtypeStruct(piece.shape, BF16) for piece in window],
        in_specs=[smem] * 3 + [hbm] * (2 + SHARDS),
        out_specs=[vmem] * (places_out + SHARDS),
        scratch_shapes=[
            pltpu.VMEM((tokens, query_width), BF16),
            pltpu.VMEM((tokens, query_width), BF16),
            pltpu.VMEM((tokens, query_width), BF16),
            pltpu.VMEM((2, SHARDS * tokens, kv_width), BF16),
            pltpu.VMEM((2, SHARDS * tokens, kv_width), F32),
            pltpu.VMEM((SLOTS * BLOCK_TOKENS, rows), F32),
            pltpu.VMEM((SLOTS * BLOCK_TOKENS, rows), F32),
            pltpu.VMEM((SLOTS * BLOCK_TOKENS, HEAD_SIZE), BF16),
            pltpu.VMEM((SLOTS * BLOCK_TOKENS, HEAD_SIZE), BF16),
            pltpu.SemaphoreType.DMA((2 + SHARDS,)),
        ],
        compiler_params=pltpu.CompilerParams(vmem_limit_bytes=20 * 2**20),
        cost_estimate=pl.CostEstimate(
            flops=2 * 10**9, bytes_accessed=2 * 10**7, transcendentals=2 * 10**6
        ),
    )(blocks, counts, me, queries, output_gradient, *window)


def sum_kernel(me_ref, *refs):
    parts, outs = refs[:SHARDS], refs[SHARDS:]
    share = outs[0].shape[1]
    for k, out in enumerate(outs):
        rows = pl.ds(pl.multiple_of((me_ref[1] ^ k) * share, share), share)
        total = parts[0][:, rows].astype(F32)
        for part in parts[1:]:
            total = total + part[:, rows].astype(F32)
        out[...] = total.astype(BF16)


def sum_parts(me, parts, places_out):
    _, tokens, width = parts[0].shape
    vmem = pl.BlockSpec(memory_space=pltpu.VMEM)
    smem = pl.BlockSpec(memory_space=pltpu.SMEM)
    piece = jax.ShapeDtypeStruct((2, tokens // places_out, width), BF16)
    return pl.pallas_call(
        sum_kernel,
        out_shape=[piece] * places_out,
        in_specs=[smem] + [vmem] * SHARDS,
        out_specs=[vmem] * places_out,
        compiler_params=pltpu.CompilerParams(vmem_limit_bytes=8 * 2**20),
    )(me, *parts)


def assemble_kernel(heads, places_out, me_ref, *refs):
    n = heads * places_out
    dq_pieces, dkv_pieces = refs[:n], refs[n : 2 * n]
    dq_out, dk_out, dv_out, sems = refs[2 * n :]
    copies = []
    for head in range(heads):
        for k in range(places_out):
            index = head * places_out + k
            place = (me_ref[1] ^ k) * heads + head
            for which, (out, source) in enumerate(
                (
                    (dq_out, dq_pieces[index]),
                    (dk_out, dkv_pieces[index].at[0]),
                    (dv_out, dkv_pieces[index].at[1]),
                )
            ):
                width = source.shape[1]
                columns = pl.ds(pl.multiple_of(place * width, width), width)
                copies.append(
                    pltpu.make_async_copy(source, out.at[:, columns], sems.at[which, index])
                )
    for copy in copies:
        copy.start()
    for copy in copies:
        copy.wait()


def assemble(me, dq_pieces, dkv_pieces, heads, places_out):
    share, query_width = dq_pieces[0].shape
    kv_width = dkv_pieces[0].shape[2]
    n = heads * places_out
    vmem = pl.BlockSpec(memory_space=pltpu.VMEM)
    hbm = pl.BlockSpec(memory_space=pl.ANY)
    smem = pl.BlockSpec(memory_space=pltpu.SMEM)
    return pl.pallas_call(
        functools.partial(assemble_kernel, heads, places_out),
        out_shape=[
            jax.ShapeDtypeStruct((share, n * query_width), BF16),
            jax.ShapeDtypeStruct((share, n * kv_width), BF16),
            jax.ShapeDtypeStruct((share, n * kv_width), BF16),
        ],
        in_specs=[smem] + [vmem] * (2 * n),
        out_specs=[hbm] * 3,
        scratch_shapes=[pltpu.SemaphoreType.DMA((3, n))],
        compiler_params=pltpu.CompilerParams(vmem_limit_bytes=8 * 2**20),
    )(me, *dq_pieces, *dkv_pieces)


def from_behind(x, by):
    size = lax.axis_size("ctx")
    return lax.ppermute(x, "ctx", [(i, (i + by) % size) for i in range(size)])


def exchange(pieces):
    return [
        piece if k == 0 else lax.ppermute(piece, "head", [(i, i ^ k) for i in range(len(pieces))])
        for k, piece in enumerate(pieces)
    ]


def on_device(queries, keys, values, output_gradient, blocks, counts):
    tokens = queries.shape[0]
    cycle_blocks = lax.axis_size("ctx") * (tokens // BLOCK_TOKENS)
    places_out = lax.axis_size("head")
    me = jnp.stack([lax.axis_index("ctx"), lax.axis_index("head")])
    heads = keys.shape[1] // HEAD_SIZE
    offsets = range(-REACH, REACH + 1)

    windows = []
    for head in range(heads):
        columns = slice(head * HEAD_SIZE, (head + 1) * HEAD_SIZE)
        own = jnp.stack([keys[:, columns], values[:, columns]])
        windows.append([own if o == 0 else from_behind(own, -o) for o in offsets])
    dq_pieces, dkv_pieces = [], []
    for head, window in enumerate(windows):
        outs = attention(
            head,
            heads,
            cycle_blocks,
            places_out,
            blocks,
            counts,
            me,
            queries,
            output_gradient,
            window,
        )
        dqueries, partials = outs[:places_out], outs[places_out:]
        parts = [p if o == 0 else from_behind(p, o) for o, p in zip(offsets, partials)]
        dq_pieces += exchange(dqueries)
        dkv_pieces += exchange(sum_parts(me, parts, places_out))
    return tuple(assemble(me, dq_pieces, dkv_pieces, heads, places_out))


def solution(mesh):
    return jax.shard_map(
        on_device,
        mesh=mesh,
        in_specs=(
            P("ctx", "head"),
            P("ctx", "head"),
            P("ctx", "head"),
            P("ctx", "head"),
            P("ctx", None),
            P("ctx"),
        ),
        out_specs=(P(("ctx", "head"), None), P(("ctx", "head"), None), P(("ctx", "head"), None)),
        check_vma=False,
    )
```

```python
import functools
import math

import jax
import jax.numpy as jnp
from jax import lax
from jax.experimental import pallas as pl
from jax.experimental.pallas import tpu as pltpu
from jax.sharding import PartitionSpec as P

HEAD_SIZE = 128
BLOCK_TOKENS = 128
SLOTS = 8
REACH = 2
SHARDS = 2 * REACH + 1
F32 = jnp.float32
BF16 = jnp.bfloat16
ROWS_BY_ROWS = (((1,), (1,)), ((), ()))
COLS_BY_COLS = (((0,), (0,)), ((), ()))
MIB = 2**20

VMEM = pl.BlockSpec(memory_space=pltpu.VMEM)
SMEM = pl.BlockSpec(memory_space=pltpu.SMEM)
HBM = pl.BlockSpec(memory_space=pltpu.HBM)
ANY = pl.BlockSpec(memory_space=pl.ANY)

BEHIND, CROSS, OWN, OTHER, AHEAD = range(SHARDS)


def attention_kernel(cycle_blocks, places_out, *refs):
    blocks_ref, counts_ref, me_ref, queries, outgrad = refs[:5]
    refs = refs[5:]
    window_hbm, refs = refs[:SHARDS], refs[SHARDS:]
    dqueries_refs, refs = refs[:places_out], refs[places_out:]
    outs, refs = refs[:SHARDS], refs[SHARDS:]
    window, sums, scores_ref, dprobs_ref = refs[:4]
    block_keys, block_values, dqueries_ref, sems = refs[4:]
    tokens, query_width = dqueries_ref.shape
    group = query_width // HEAD_SIZE
    own_blocks, rows = tokens // BLOCK_TOKENS, group * BLOCK_TOKENS
    scale = 1.0 / math.sqrt(HEAD_SIZE)
    scale_log2 = scale * math.log2(math.e)

    copies = []
    for j in range(SHARDS):
        place = window.at[:, pl.ds(j * tokens, tokens), :]
        copies.append(pltpu.make_async_copy(window_hbm[j], place, sems.at[j]))
    for copy in copies:
        copy.start()
    sums[...] = jnp.zeros_like(sums)
    for copy in copies:
        copy.wait()
    half = cycle_blocks // 2
    me_block = me_ref[0] * own_blocks
    mirrored = me_ref[0] % 2 == 1

    def query_block(qblock, live):
        row_ds = pl.ds(pl.multiple_of(qblock * BLOCK_TOKENS, BLOCK_TOKENS), BLOCK_TOKENS)
        q_cols = [slice(g * HEAD_SIZE, (g + 1) * HEAD_SIZE) for g in range(group)]
        slots = [slice(s * BLOCK_TOKENS, (s + 1) * BLOCK_TOKENS) for s in range(live)]
        places = []
        for s in range(live):
            ahead = lax.rem(blocks_ref[qblock, s] - me_block + half + cycle_blocks, cycle_blocks)
            place = ahead - half + REACH * own_blocks
            shard = lax.div(place, own_blocks)
            flipped = place + (2 * REACH - 2 * shard) * own_blocks
            place = jnp.where(mirrored, flipped, place)
            place = pl.ds(pl.multiple_of(place * BLOCK_TOKENS, BLOCK_TOKENS), BLOCK_TOKENS)
            places.append(place)
            block_keys[slots[s]] = window[0, place]
            block_values[slots[s]] = window[1, place]
        q_ds = pl.ds(pl.multiple_of(qblock * rows, rows), rows)
        q, o = queries[q_ds], outgrad[q_ds]

        def fold(x, op):
            return op(x.reshape(BLOCK_TOKENS // 8, 8, rows), axis=0)

        top = None
        for s in range(live):
            scores = lax.dot_general(
                block_keys[slots[s]], q, ROWS_BY_ROWS, preferred_element_type=F32
            )
            scores_ref[slots[s]] = scores
            part = fold(scores, jnp.max)
            top = part if s == 0 else jnp.maximum(top, part)
        row_max = jnp.max(top, axis=0, keepdims=True) * scale_log2
        total = weighted = None
        for s in range(live):
            dprobs = lax.dot_general(
                block_values[slots[s]], o, ROWS_BY_ROWS, preferred_element_type=F32
            )
            weights = jnp.exp2(scores_ref[slots[s]] * scale_log2 - row_max)
            dprobs_ref[slots[s]] = dprobs
            scores_ref[slots[s]] = weights
            part, wpart = fold(weights, jnp.sum), fold(weights * dprobs, jnp.sum)
            total = part if s == 0 else total + part
            weighted = wpart if s == 0 else weighted + wpart
        inverse = 1.0 / jnp.sum(total, axis=0, keepdims=True)
        row_delta = jnp.sum(weighted, axis=0, keepdims=True) * inverse
        dq = None
        for s in range(live):
            probs = scores_ref[slots[s]] * inverse
            dscores = (probs * (dprobs_ref[slots[s]] - row_delta)).astype(BF16)
            sums[0, places[s]] += jnp.dot(dscores, q, preferred_element_type=F32)
            sums[1, places[s]] += jnp.dot(probs.astype(BF16), o, preferred_element_type=F32)
            part = lax.dot_general(
                block_keys[slots[s]], dscores, COLS_BY_COLS, preferred_element_type=F32
            )
            dq = part if s == 0 else dq + part
        dq = jnp.transpose(dq * scale).astype(BF16)
        for g in range(group):
            dqueries_ref[row_ds, q_cols[g]] = dq[g * BLOCK_TOKENS : (g + 1) * BLOCK_TOKENS]

    def one_block(qblock, carry):
        for live in range(1, SLOTS + 1):
            pl.when(counts_ref[qblock] == live)(functools.partial(query_block, qblock, live))
        return carry

    lax.fori_loop(0, own_blocks, one_block, 0)
    share = tokens // places_out
    for k in range(places_out):
        first = pl.multiple_of((me_ref[1] ^ k) * share, share)
        dqueries_refs[k][0] = dqueries_ref[pl.ds(first, share)]
    for j, out in enumerate(outs):
        span = slice(j * tokens, (j + 1) * tokens)
        out[0] = (sums[0, span] * scale).astype(BF16)
        out[1] = sums[1, span].astype(BF16)


def attention(cycle_blocks, places_out, scalars, queries, outgrad, window):
    tokens = window[OWN].shape[1]
    query_width = queries.shape[0] // tokens * HEAD_SIZE
    rows = query_width // HEAD_SIZE * BLOCK_TOKENS
    part = (2, tokens, HEAD_SIZE)
    piece = (1, tokens // places_out, query_width)
    shapes = [piece] * places_out + [part] * SHARDS
    keys_rows = SLOTS * BLOCK_TOKENS
    return pl.pallas_call(
        functools.partial(attention_kernel, cycle_blocks, places_out),
        out_shape=[jax.ShapeDtypeStruct(shape, BF16) for shape in shapes],
        in_specs=[SMEM] * 3 + [VMEM] * 2 + [ANY] * SHARDS,
        out_specs=[VMEM] * len(shapes),
        scratch_shapes=[
            pltpu.VMEM((2, SHARDS * tokens, HEAD_SIZE), BF16),
            pltpu.VMEM((2, SHARDS * tokens, HEAD_SIZE), F32),
            pltpu.VMEM((keys_rows, rows), F32),
            pltpu.VMEM((keys_rows, rows), F32),
            pltpu.VMEM((keys_rows, HEAD_SIZE), BF16),
            pltpu.VMEM((keys_rows, HEAD_SIZE), BF16),
            pltpu.VMEM((tokens, query_width), BF16),
            pltpu.SemaphoreType.DMA((SHARDS,)),
        ],
        compiler_params=pltpu.CompilerParams(vmem_limit_bytes=24 * MIB),
        cost_estimate=pl.CostEstimate(
            flops=10**10, bytes_accessed=2 * 10**7, transcendentals=2 * 10**6
        ),
    )(*scalars, queries, outgrad, *window)


def arrange_kernel(heads, queries_hbm, outgrad_hbm, *refs):
    outs, sems = refs[: 2 * heads], refs[2 * heads]
    tokens, query_width = queries_hbm.shape
    group = query_width // heads // HEAD_SIZE
    copies = []
    for head in range(heads):
        for i, source in enumerate((queries_hbm, outgrad_hbm)):
            for block in range(tokens // BLOCK_TOKENS):
                for g in range(group):
                    rows = pl.ds(block * BLOCK_TOKENS, BLOCK_TOKENS)
                    columns = pl.ds((head * group + g) * HEAD_SIZE, HEAD_SIZE)
                    to = pl.ds((block * group + g) * BLOCK_TOKENS, BLOCK_TOKENS)
                    copies.append(
                        pltpu.make_async_copy(
                            source.at[rows, columns],
                            outs[2 * head + i].at[to],
                            sems.at[head, i, block, g],
                        )
                    )
    for copy in copies:
        copy.start()
    for copy in copies:
        copy.wait()


def arrange(heads, queries, outgrad):
    tokens, query_width = queries.shape
    group = query_width // heads // HEAD_SIZE
    out = jax.ShapeDtypeStruct((tokens * group, HEAD_SIZE), BF16)
    outs = pl.pallas_call(
        functools.partial(arrange_kernel, heads),
        out_shape=[out] * (2 * heads),
        in_specs=[HBM] * 2,
        out_specs=[VMEM] * (2 * heads),
        scratch_shapes=[pltpu.SemaphoreType.DMA((heads, 2, tokens // BLOCK_TOKENS, group))],
        compiler_params=pltpu.CompilerParams(vmem_limit_bytes=8 * MIB),
        cost_estimate=pl.CostEstimate(flops=0, bytes_accessed=8 * MIB, transcendentals=0),
    )(queries, outgrad)
    return [outs[2 * head : 2 * head + 2] for head in range(heads)]


def pack_kernel(heads, keys_hbm, values_hbm, *refs):
    outs, sems = refs[:heads], refs[heads]
    copies = []
    for head, out in enumerate(outs):
        columns = pl.ds(head * HEAD_SIZE, HEAD_SIZE)
        for i, source in enumerate((keys_hbm, values_hbm)):
            copies.append(
                pltpu.make_async_copy(source.at[:, columns], out.at[i], sems.at[head, i])
            )
    for copy in copies:
        copy.start()
    for copy in copies:
        copy.wait()


def pack(keys, values):
    heads = keys.shape[1] // HEAD_SIZE
    return pl.pallas_call(
        functools.partial(pack_kernel, heads),
        out_shape=[jax.ShapeDtypeStruct((2, keys.shape[0], HEAD_SIZE), BF16)] * heads,
        in_specs=[HBM] * 2,
        out_specs=[VMEM] * heads,
        scratch_shapes=[pltpu.SemaphoreType.DMA((heads, 2))],
        compiler_params=pltpu.CompilerParams(vmem_limit_bytes=56 * MIB),
    )(keys, values)


def sum_kernel(heads, places_out, me_ref, *refs):
    outs = refs[4 * heads :]
    share = outs[0].shape[2]
    for k, out in enumerate(outs):
        rows = pl.ds(pl.multiple_of((me_ref[1] ^ k) * share, share), share)
        for head in range(heads):
            parts = [part[:, rows].astype(F32) for part in refs[4 * head : 4 * head + 4]]
            out[head] = ((parts[0] + parts[1]) + (parts[2] + parts[3])).astype(BF16)


def sum_parts(me, parts, places_out):
    heads = len(parts) // 4
    _, tokens, width = parts[0].shape
    piece = jax.ShapeDtypeStruct((heads, 2, tokens // places_out, width), BF16)
    return pl.pallas_call(
        functools.partial(sum_kernel, heads, places_out),
        out_shape=[piece] * places_out,
        in_specs=[SMEM] + [VMEM] * len(parts),
        out_specs=[VMEM] * places_out,
        compiler_params=pltpu.CompilerParams(vmem_limit_bytes=8 * MIB),
    )(me, *parts)


def assemble_kernel(places_out, n_outs, me_ref, *refs):
    pieces, outs, sems = refs[: -n_outs - 1], refs[-n_outs - 1 : -1], refs[-1]
    per, width = pieces[0].shape[0], pieces[0].shape[-1]
    heads = len(pieces) // places_out * per
    copies = []
    for index, piece in enumerate(pieces):
        for part in range(per):
            head = index // places_out * per + part
            place = (me_ref[1] ^ (index % places_out)) * heads + head
            columns = pl.ds(pl.multiple_of(place * width, width), width)
            for i, out in enumerate(outs):
                source = piece.at[part] if n_outs == 1 else piece.at[part, i]
                copies.append(
                    pltpu.make_async_copy(source, out.at[:, columns], sems.at[i, index, part])
                )
    for copy in copies:
        copy.start()
    for copy in copies:
        copy.wait()


def assemble(me, groups, n_outs):
    places_out = len(groups[0])
    pieces = [piece for group in groups for piece in group]
    per, share, width = pieces[0].shape[0], *pieces[0].shape[-2:]
    out = jax.ShapeDtypeStruct((share, len(pieces) * per * width), BF16)
    return pl.pallas_call(
        functools.partial(assemble_kernel, places_out, n_outs),
        out_shape=[out] * n_outs,
        in_specs=[SMEM] + [VMEM] * len(pieces),
        out_specs=[ANY] * n_outs,
        scratch_shapes=[pltpu.SemaphoreType.DMA((n_outs, len(pieces), per))],
        compiler_params=pltpu.CompilerParams(vmem_limit_bytes=4 * MIB),
    )(me, *pieces)


def swap(x):
    return lax.ppermute(x, "ctx", [(i, i ^ 1) for i in range(lax.axis_size("ctx"))])


def far(x, by):
    size = lax.axis_size("ctx")
    pairs = [(i, (i + (by if i % 2 == 0 else -by)) % size) for i in range(size)]
    return lax.ppermute(x, "ctx", pairs)


def after(x, *others):
    return lax.optimization_barrier((x, *others))[0] if others else x


def exchange(pieces):
    return [
        piece if k == 0 else lax.ppermute(piece, "head", [(i, i ^ k) for i in range(len(pieces))])
        for k, piece in enumerate(pieces)
    ]


def on_device(queries, keys, values, output_gradient, blocks, counts):
    tokens = queries.shape[0]
    cycle_blocks = lax.axis_size("ctx") * (tokens // BLOCK_TOKENS)
    places_out = lax.axis_size("head")
    me = jnp.stack([lax.axis_index("ctx"), lax.axis_index("head")])
    heads = keys.shape[1] // HEAD_SIZE

    rows = arrange(heads, queries, output_gradient)
    windows = []
    for own in pack(keys, values):
        if windows:
            own = after(own, windows[-1][AHEAD])
        ahead, behind, other = far(own, -REACH), far(own, REACH), swap(own)
        crossed = swap(ahead if windows else after(ahead, *rows[0]))
        windows.append([behind, crossed, own, other, ahead])
    dq_pieces, parts, sent = [], [], ()
    for (q_rows, o_rows), window in zip(rows, windows):
        outs = attention(cycle_blocks, places_out, (blocks, counts, me), q_rows, o_rows, window)
        pieces, outs = outs[:places_out], after(outs[places_out:], *sent)
        plain, near = far(outs[BEHIND], -REACH), swap(outs[CROSS])
        joined = (outs[AHEAD].astype(F32) + near.astype(F32)).astype(BF16)
        other = swap(outs[OTHER])
        dq_pieces.append(exchange(pieces))
        sent = (near, plain, other)
        parts += [outs[OWN], other, plain, far(joined, REACH)]
    (dqueries,) = assemble(me, dq_pieces, 1)
    dkv_pieces = exchange(sum_parts(me, parts, places_out))
    dkeys, dvalues = assemble(me, [dkv_pieces], 2)
    return dqueries, dkeys, dvalues


def solution(mesh):
    return jax.shard_map(
        on_device,
        mesh=mesh,
        in_specs=(
            P("ctx", "head"),
            P("ctx", "head"),
            P("ctx", "head"),
            P("ctx", "head"),
            P("ctx", None),
            P("ctx"),
        ),
        out_specs=(P(("ctx", "head"), None), P(("ctx", "head"), None), P(("ctx", "head"), None)),
        check_vma=False,
    )
```

```python
import functools
import math

import jax
import jax.numpy as jnp
from jax import lax
from jax.experimental import pallas as pl
from jax.experimental.pallas import tpu as pltpu
from jax.sharding import PartitionSpec as P

HEAD_SIZE = 128
BLOCK_TOKENS = 128
SLOTS = 8
REACH = 2
SHARDS = 2 * REACH + 1
F32 = jnp.float32
BF16 = jnp.bfloat16
ROWS_BY_ROWS = (((1,), (1,)), ((), ()))
COLS_BY_COLS = (((0,), (0,)), ((), ()))
MIB = 2**20

VMEM = pl.BlockSpec(memory_space=pltpu.VMEM)
SMEM = pl.BlockSpec(memory_space=pltpu.SMEM)
HBM = pl.BlockSpec(memory_space=pltpu.HBM)
ANY = pl.BlockSpec(memory_space=pl.ANY)

BEHIND, CROSS, OWN, OTHER, AHEAD = range(SHARDS)


def attention_kernel(head, cycle_blocks, places_out, *refs):
    blocks_ref, counts_ref, me_ref, queries, outgrad = refs[:5]
    window_hbm, refs = refs[5 : 5 + SHARDS], refs[5 + SHARDS :]
    if head > 0:
        before, refs = refs[:places_out], refs[places_out:]
    dqueries_refs, refs = refs[:places_out], refs[places_out:]
    outs, refs = refs[:SHARDS], refs[SHARDS:]
    window, sums, scores_ref, dprobs_ref = refs[:4]
    block_keys, block_values, dqueries_ref, sems = refs[4:]
    tokens, query_width = dqueries_ref.shape
    group = query_width // HEAD_SIZE
    own_blocks, rows = tokens // BLOCK_TOKENS, group * BLOCK_TOKENS
    scale = 1.0 / math.sqrt(HEAD_SIZE)
    scale_log2 = scale * math.log2(math.e)

    copies = []
    for j in range(SHARDS):
        place = window.at[:, pl.ds(j * tokens, tokens), :]
        copies.append(pltpu.make_async_copy(window_hbm[j], place, sems.at[j]))
    for copy in copies:
        copy.start()
    sums[...] = jnp.zeros_like(sums)
    for copy in copies:
        copy.wait()
    half = cycle_blocks // 2
    me_block = me_ref[0] * own_blocks
    mirrored = me_ref[0] % 2 == 1

    def query_block(qblock, live):
        row_ds = pl.ds(pl.multiple_of(qblock * BLOCK_TOKENS, BLOCK_TOKENS), BLOCK_TOKENS)
        q_cols = [slice(g * HEAD_SIZE, (g + 1) * HEAD_SIZE) for g in range(group)]
        slots = [slice(s * BLOCK_TOKENS, (s + 1) * BLOCK_TOKENS) for s in range(live)]
        places = []
        for s in range(live):
            ahead = lax.rem(blocks_ref[qblock, s] - me_block + half + cycle_blocks, cycle_blocks)
            place = ahead - half + REACH * own_blocks
            shard = lax.div(place, own_blocks)
            flipped = place + (2 * REACH - 2 * shard) * own_blocks
            place = jnp.where(mirrored, flipped, place)
            place = pl.ds(pl.multiple_of(place * BLOCK_TOKENS, BLOCK_TOKENS), BLOCK_TOKENS)
            places.append(place)
            block_keys[slots[s]] = window[0, place]
            block_values[slots[s]] = window[1, place]
        q_ds = pl.ds(pl.multiple_of(qblock * rows, rows), rows)
        q, o = queries[q_ds], outgrad[q_ds]

        def fold(x, op):
            return op(x.reshape(BLOCK_TOKENS // 8, 8, rows), axis=0)

        top = None
        for s in range(live):
            scores = lax.dot_general(
                block_keys[slots[s]], q, ROWS_BY_ROWS, preferred_element_type=F32
            )
            scores_ref[slots[s]] = scores
            part = fold(scores, jnp.max)
            top = part if s == 0 else jnp.maximum(top, part)
        row_max = jnp.max(top, axis=0, keepdims=True) * scale_log2
        total = weighted = None
        for s in range(live):
            dprobs = lax.dot_general(
                block_values[slots[s]], o, ROWS_BY_ROWS, preferred_element_type=F32
            )
            weights = jnp.exp2(scores_ref[slots[s]] * scale_log2 - row_max)
            dprobs_ref[slots[s]] = dprobs
            scores_ref[slots[s]] = weights
            part, wpart = fold(weights, jnp.sum), fold(weights * dprobs, jnp.sum)
            total = part if s == 0 else total + part
            weighted = wpart if s == 0 else weighted + wpart
        inverse = 1.0 / jnp.sum(total, axis=0, keepdims=True)
        row_delta = jnp.sum(weighted, axis=0, keepdims=True) * inverse
        dq = None
        for s in range(live):
            probs = scores_ref[slots[s]] * inverse
            dscores = (probs * (dprobs_ref[slots[s]] - row_delta)).astype(BF16)
            sums[0, places[s]] += jnp.dot(dscores, q, preferred_element_type=F32)
            sums[1, places[s]] += jnp.dot(probs.astype(BF16), o, preferred_element_type=F32)
            part = lax.dot_general(
                block_keys[slots[s]], dscores, COLS_BY_COLS, preferred_element_type=F32
            )
            dq = part if s == 0 else dq + part
        dq = jnp.transpose(dq * scale).astype(BF16)
        for g in range(group):
            dqueries_ref[row_ds, q_cols[g]] = dq[g * BLOCK_TOKENS : (g + 1) * BLOCK_TOKENS]

    def one_block(qblock, carry):
        for live in range(1, SLOTS + 1):
            pl.when(counts_ref[qblock] == live)(functools.partial(query_block, qblock, live))
        return carry

    lax.fori_loop(0, own_blocks, one_block, 0)
    share = tokens // places_out
    for k, out in enumerate(dqueries_refs):
        if head > 0:
            out[:head] = before[k][...]
        first = pl.multiple_of((me_ref[1] ^ k) * share, share)
        out[head] = dqueries_ref[pl.ds(first, share)]
    for j, out in enumerate(outs):
        span = slice(j * tokens, (j + 1) * tokens)
        out[0] = (sums[0, span] * scale).astype(BF16)
        out[1] = sums[1, span].astype(BF16)


def attention(head, cycle_blocks, places_out, scalars, queries, outgrad, window, before):
    tokens = window[OWN].shape[1]
    query_width = queries.shape[0] // tokens * HEAD_SIZE
    rows = query_width // HEAD_SIZE * BLOCK_TOKENS
    part = (2, tokens, HEAD_SIZE)
    shapes = [(head + 1, tokens // places_out, query_width)] * places_out + [part] * SHARDS
    keys_rows = SLOTS * BLOCK_TOKENS
    outs = pl.pallas_call(
        functools.partial(attention_kernel, head, cycle_blocks, places_out),
        out_shape=[jax.ShapeDtypeStruct(shape, BF16) for shape in shapes],
        in_specs=[SMEM] * 3 + [VMEM] * 2 + [ANY] * SHARDS + [VMEM] * len(before),
        out_specs=[VMEM] * len(shapes),
        scratch_shapes=[
            pltpu.VMEM((2, SHARDS * tokens, HEAD_SIZE), BF16),
            pltpu.VMEM((2, SHARDS * tokens, HEAD_SIZE), F32),
            pltpu.VMEM((keys_rows, rows), F32),
            pltpu.VMEM((keys_rows, rows), F32),
            pltpu.VMEM((keys_rows, HEAD_SIZE), BF16),
            pltpu.VMEM((keys_rows, HEAD_SIZE), BF16),
            pltpu.VMEM((tokens, query_width), BF16),
            pltpu.SemaphoreType.DMA((SHARDS,)),
        ],
        compiler_params=pltpu.CompilerParams(vmem_limit_bytes=24 * MIB),
        cost_estimate=pl.CostEstimate(
            flops=10**10, bytes_accessed=2 * 10**7, transcendentals=2 * 10**6
        ),
    )(*scalars, queries, outgrad, *window, *before)
    return outs[:places_out], outs[places_out:]


def arrange_kernel(heads, queries_hbm, outgrad_hbm, *refs):
    outs, sems = refs[: 2 * heads], refs[2 * heads]
    tokens, query_width = queries_hbm.shape
    group = query_width // heads // HEAD_SIZE
    copies = []
    for head in range(heads):
        for i, source in enumerate((queries_hbm, outgrad_hbm)):
            for block in range(tokens // BLOCK_TOKENS):
                for g in range(group):
                    rows = pl.ds(block * BLOCK_TOKENS, BLOCK_TOKENS)
                    columns = pl.ds((head * group + g) * HEAD_SIZE, HEAD_SIZE)
                    to = pl.ds((block * group + g) * BLOCK_TOKENS, BLOCK_TOKENS)
                    copies.append(
                        pltpu.make_async_copy(
                            source.at[rows, columns],
                            outs[2 * head + i].at[to],
                            sems.at[head, i, block, g],
                        )
                    )
    for copy in copies:
        copy.start()
    for copy in copies:
        copy.wait()


def arrange(heads, queries, outgrad):
    tokens, query_width = queries.shape
    group = query_width // heads // HEAD_SIZE
    out = jax.ShapeDtypeStruct((tokens * group, HEAD_SIZE), BF16)
    outs = pl.pallas_call(
        functools.partial(arrange_kernel, heads),
        out_shape=[out] * (2 * heads),
        in_specs=[HBM] * 2,
        out_specs=[VMEM] * (2 * heads),
        scratch_shapes=[pltpu.SemaphoreType.DMA((heads, 2, tokens // BLOCK_TOKENS, group))],
        compiler_params=pltpu.CompilerParams(vmem_limit_bytes=8 * MIB),
        cost_estimate=pl.CostEstimate(flops=0, bytes_accessed=8 * MIB, transcendentals=0),
    )(queries, outgrad)
    return [outs[2 * head : 2 * head + 2] for head in range(heads)]


def pack_kernel(heads, keys_hbm, values_hbm, *refs):
    outs, sems = refs[:heads], refs[heads]
    copies = []
    for head, out in enumerate(outs):
        columns = pl.ds(head * HEAD_SIZE, HEAD_SIZE)
        for i, source in enumerate((keys_hbm, values_hbm)):
            copies.append(
                pltpu.make_async_copy(source.at[:, columns], out.at[i], sems.at[head, i])
            )
    for copy in copies:
        copy.start()
    for copy in copies:
        copy.wait()


def pack(keys, values):
    heads = keys.shape[1] // HEAD_SIZE
    return pl.pallas_call(
        functools.partial(pack_kernel, heads),
        out_shape=[jax.ShapeDtypeStruct((2, keys.shape[0], HEAD_SIZE), BF16)] * heads,
        in_specs=[HBM] * 2,
        out_specs=[VMEM] * heads,
        scratch_shapes=[pltpu.SemaphoreType.DMA((heads, 2))],
        compiler_params=pltpu.CompilerParams(vmem_limit_bytes=56 * MIB),
    )(keys, values)


def sum_kernel(heads, places_out, me_ref, *refs):
    outs = refs[4 * heads :]
    share = outs[0].shape[2]
    for k, out in enumerate(outs):
        rows = pl.ds(pl.multiple_of((me_ref[1] ^ k) * share, share), share)
        for head in range(heads):
            parts = [part[:, rows].astype(F32) for part in refs[4 * head : 4 * head + 4]]
            out[head] = ((parts[0] + parts[1]) + (parts[2] + parts[3])).astype(BF16)


def sum_parts(me, parts, places_out):
    heads = len(parts) // 4
    _, tokens, width = parts[0].shape
    piece = jax.ShapeDtypeStruct((heads, 2, tokens // places_out, width), BF16)
    return pl.pallas_call(
        functools.partial(sum_kernel, heads, places_out),
        out_shape=[piece] * places_out,
        in_specs=[SMEM] + [VMEM] * len(parts),
        out_specs=[VMEM] * places_out,
        compiler_params=pltpu.CompilerParams(vmem_limit_bytes=8 * MIB),
    )(me, *parts)


def assemble_kernel(places_out, n_outs, me_ref, *refs):
    pieces, outs, sems = refs[: -n_outs - 1], refs[-n_outs - 1 : -1], refs[-1]
    per, width = pieces[0].shape[0], pieces[0].shape[-1]
    heads = len(pieces) // places_out * per
    copies = []
    for index, piece in enumerate(pieces):
        for part in range(per):
            head = index // places_out * per + part
            place = (me_ref[1] ^ (index % places_out)) * heads + head
            columns = pl.ds(pl.multiple_of(place * width, width), width)
            for i, out in enumerate(outs):
                source = piece.at[part] if n_outs == 1 else piece.at[part, i]
                copies.append(
                    pltpu.make_async_copy(source, out.at[:, columns], sems.at[i, index, part])
                )
    for copy in copies:
        copy.start()
    for copy in copies:
        copy.wait()


def assemble(me, groups, n_outs):
    places_out = len(groups[0])
    pieces = [piece for group in groups for piece in group]
    per, share, width = pieces[0].shape[0], *pieces[0].shape[-2:]
    out = jax.ShapeDtypeStruct((share, len(pieces) * per * width), BF16)
    return pl.pallas_call(
        functools.partial(assemble_kernel, places_out, n_outs),
        out_shape=[out] * n_outs,
        in_specs=[SMEM] + [VMEM] * len(pieces),
        out_specs=[ANY] * n_outs,
        scratch_shapes=[pltpu.SemaphoreType.DMA((n_outs, len(pieces), per))],
        compiler_params=pltpu.CompilerParams(vmem_limit_bytes=4 * MIB),
    )(me, *pieces)


def swap(x):
    return lax.ppermute(x, "ctx", [(i, i ^ 1) for i in range(lax.axis_size("ctx"))])


def far_place(i, by, size):
    return (i + (by if i % 2 == 0 else -by)) % size


def far(x, by):
    size = lax.axis_size("ctx")
    return lax.ppermute(x, "ctx", [(i, far_place(i, by, size)) for i in range(size)])


def after(x, *others):
    return lax.optimization_barrier((x, *others))[0] if others else x


def exchange(pieces):
    return [
        piece if k == 0 else lax.ppermute(piece, "head", [(i, i ^ k) for i in range(len(pieces))])
        for k, piece in enumerate(pieces)
    ]


def on_device(queries, keys, values, output_gradient, blocks, counts):
    tokens = queries.shape[0]
    cycle_blocks = lax.axis_size("ctx") * (tokens // BLOCK_TOKENS)
    places_out = lax.axis_size("head")
    me = jnp.stack([lax.axis_index("ctx"), lax.axis_index("head")])
    heads = keys.shape[1] // HEAD_SIZE

    rows = arrange(heads, queries, output_gradient)
    windows = []
    for own in pack(keys, values):
        if windows:
            own = after(own, windows[-1][AHEAD])
        ahead, behind, other = far(own, -REACH), far(own, REACH), swap(own)
        crossed = swap(ahead if windows else after(ahead, *rows[0]))
        windows.append([behind, crossed, own, other, ahead])
    dq, parts, sent = [], [], ()
    for head, ((q_rows, o_rows), window) in enumerate(zip(rows, windows)):
        dq, outs = attention(
            head, cycle_blocks, places_out, (blocks, counts, me), q_rows, o_rows, window, dq
        )
        outs = after(outs, *sent)
        plain, near = far(outs[BEHIND], -REACH), swap(outs[CROSS])
        joined = (outs[AHEAD].astype(F32) + near.astype(F32)).astype(BF16)
        other = swap(outs[OTHER])
        sent = (near, plain, other)
        parts += [outs[OWN], other, plain, far(joined, REACH)]
    (dqueries,) = assemble(me, [exchange(dq)], 1)
    dkv_pieces = exchange(sum_parts(me, parts, places_out))
    dkeys, dvalues = assemble(me, [dkv_pieces], 2)
    return dqueries, dkeys, dvalues


def solution(mesh):
    return jax.shard_map(
        on_device,
        mesh=mesh,
        in_specs=(
            P("ctx", "head"),
            P("ctx", "head"),
            P("ctx", "head"),
            P("ctx", "head"),
            P("ctx", None),
            P("ctx"),
        ),
        out_specs=(P(("ctx", "head"), None), P(("ctx", "head"), None), P(("ctx", "head"), None)),
        check_vma=False,
    )
```

```python
import functools
import math

import jax
import jax.numpy as jnp
from jax import lax
from jax.experimental import pallas as pl
from jax.experimental.pallas import tpu as pltpu
from jax.sharding import PartitionSpec as P

HEAD_SIZE = 128
BLOCK_TOKENS = 128
SLOTS = 8
REACH = 2
SHARDS = 2 * REACH + 1
F32 = jnp.float32
BF16 = jnp.bfloat16
ROWS_BY_ROWS = (((1,), (1,)), ((), ()))
COLS_BY_COLS = (((0,), (0,)), ((), ()))
MIB = 2**20
ABOVE = 64.0

VMEM = pl.BlockSpec(memory_space=pltpu.VMEM)
SMEM = pl.BlockSpec(memory_space=pltpu.SMEM)
HBM = pl.BlockSpec(memory_space=pltpu.HBM)
ANY = pl.BlockSpec(memory_space=pl.ANY)

BEHIND, CROSS, OWN, OTHER, AHEAD = range(SHARDS)


def attention_kernel(head, cycle_blocks, places_out, *refs):
    blocks_ref, counts_ref, me_ref, queries, outgrad = refs[:5]
    window_hbm, refs = refs[5 : 5 + SHARDS], refs[5 + SHARDS :]
    if head > 0:
        before, refs = refs[:places_out], refs[places_out:]
    dqueries_refs, refs = refs[:places_out], refs[places_out:]
    outs, refs = refs[:SHARDS], refs[SHARDS:]
    window, sums, scores_ref, dprobs_ref = refs[:4]
    block_keys, block_values, dqueries_ref, above_ref, dq_ref, sems = refs[4:]
    tokens, query_width = dqueries_ref.shape
    group = query_width // HEAD_SIZE
    own_blocks, rows = tokens // BLOCK_TOKENS, group * BLOCK_TOKENS
    scale = 1.0 / math.sqrt(HEAD_SIZE)
    scale_log2 = scale * math.log2(math.e)

    copies = []
    for j in range(SHARDS):
        place = window.at[:, pl.ds(j * tokens, tokens), :]
        copies.append(pltpu.make_async_copy(window_hbm[j], place, sems.at[j]))
    for copy in copies:
        copy.start()
    sums[...] = jnp.zeros_like(sums)
    for copy in copies:
        copy.wait()
    half = cycle_blocks // 2
    me_block = me_ref[0] * own_blocks
    mirrored = me_ref[0] % 2 == 1

    def window_place(qblock, s):
        ahead = lax.rem(blocks_ref[qblock, s] - me_block + half + cycle_blocks, cycle_blocks)
        place = ahead - half + REACH * own_blocks
        shard = lax.div(place, own_blocks)
        flipped = place + (2 * REACH - 2 * shard) * own_blocks
        place = jnp.where(mirrored, flipped, place)
        return pl.ds(pl.multiple_of(place * BLOCK_TOKENS, BLOCK_TOKENS), BLOCK_TOKENS)

    def query_block(qblock, live):
        row_ds = pl.ds(pl.multiple_of(qblock * BLOCK_TOKENS, BLOCK_TOKENS), BLOCK_TOKENS)
        q_cols = [slice(g * HEAD_SIZE, (g + 1) * HEAD_SIZE) for g in range(group)]
        slots = [slice(s * BLOCK_TOKENS, (s + 1) * BLOCK_TOKENS) for s in range(live)]
        places = []
        for s in range(live):
            place = window_place(qblock, s)
            places.append(place)
            block_keys[slots[s]] = window[0, place]
            block_values[slots[s]] = window[1, place]
        q_ds = pl.ds(pl.multiple_of(qblock * rows, rows), rows)
        q, o = queries[q_ds], outgrad[q_ds]

        def fold(x, op):
            return op(x.reshape(BLOCK_TOKENS // 8, 8, rows), axis=0)

        total = weighted = top = None
        for s in range(live):
            scores = lax.dot_general(
                block_keys[slots[s]], q, ROWS_BY_ROWS, preferred_element_type=F32
            )
            top = fold(scores, jnp.max) if s == 0 else jnp.maximum(top, fold(scores, jnp.max))
            if s == 0:
                shift = jnp.max(top, axis=0, keepdims=True) * scale_log2
            dprobs = lax.dot_general(
                block_values[slots[s]], o, ROWS_BY_ROWS, preferred_element_type=F32
            )
            weights = jnp.exp2(scores * scale_log2 - shift)
            dprobs_ref[slots[s]] = dprobs
            scores_ref[slots[s]] = weights
            part, wpart = fold(weights, jnp.sum), fold(weights * dprobs, jnp.sum)
            total = part if s == 0 else total + part
            weighted = wpart if s == 0 else weighted + wpart
        above_ref[...] = jnp.maximum(above_ref[...], top * scale_log2 - shift)
        inverse = 1.0 / jnp.sum(total, axis=0, keepdims=True)
        row_delta = jnp.sum(weighted, axis=0, keepdims=True) * inverse
        dq = None
        for s in range(live):
            probs = scores_ref[slots[s]] * inverse
            dscores = (probs * (dprobs_ref[slots[s]] - row_delta)).astype(BF16)
            sums[0, places[s]] += jnp.dot(dscores, q, preferred_element_type=F32)
            sums[1, places[s]] += jnp.dot(probs.astype(BF16), o, preferred_element_type=F32)
            part = lax.dot_general(
                block_keys[slots[s]], dscores, COLS_BY_COLS, preferred_element_type=F32
            )
            dq = part if s == 0 else dq + part
        dq = jnp.transpose(dq * scale).astype(BF16)
        for g in range(group):
            dqueries_ref[row_ds, q_cols[g]] = dq[g * BLOCK_TOKENS : (g + 1) * BLOCK_TOKENS]

    def one_block(qblock, carry):
        count = counts_ref[qblock]

        def among(least, most):
            if least == most:
                return functools.partial(query_block, qblock, least)
            middle = (least + most) // 2
            return lambda: lax.cond(count <= middle, among(least, middle), among(middle + 1, most))

        among(1, SLOTS)()
        return carry

    def careful_block(qblock, carry):
        row_ds = pl.ds(pl.multiple_of(qblock * BLOCK_TOKENS, BLOCK_TOKENS), BLOCK_TOKENS)
        q_ds = pl.ds(pl.multiple_of(qblock * rows, rows), rows)
        q, o = queries[q_ds], outgrad[q_ds]
        count = counts_ref[qblock]

        def fold(x, op):
            return op(x.reshape(BLOCK_TOKENS // 8, 8, rows), axis=0)

        def slot(s):
            place = window_place(qblock, s)
            return place, pl.ds(pl.multiple_of(s * BLOCK_TOKENS, BLOCK_TOKENS), BLOCK_TOKENS)

        def scores_of(s, top):
            place, to = slot(s)
            scores_ref[to] = lax.dot_general(
                window[0, place], q, ROWS_BY_ROWS, preferred_element_type=F32
            )
            return jnp.maximum(top, fold(scores_ref[to], jnp.max))

        top = lax.fori_loop(0, count, scores_of, jnp.full((8, rows), -jnp.inf, F32))
        row_max = jnp.max(top, axis=0, keepdims=True) * scale_log2

        def weights_of(s, sums_so_far):
            place, to = slot(s)
            dprobs = lax.dot_general(
                window[1, place], o, ROWS_BY_ROWS, preferred_element_type=F32
            )
            weights = jnp.exp2(scores_ref[to] * scale_log2 - row_max)
            dprobs_ref[to] = dprobs
            scores_ref[to] = weights
            total, weighted = sums_so_far
            return total + fold(weights, jnp.sum), weighted + fold(weights * dprobs, jnp.sum)

        zeros = jnp.zeros((8, rows), F32)
        total, weighted = lax.fori_loop(0, count, weights_of, (zeros, zeros))
        inverse = 1.0 / jnp.sum(total, axis=0, keepdims=True)
        row_delta = jnp.sum(weighted, axis=0, keepdims=True) * inverse
        dq_ref[...] = jnp.zeros_like(dq_ref)

        def gradients_of(s, carry):
            place, to = slot(s)
            probs = scores_ref[to] * inverse
            dscores = (probs * (dprobs_ref[to] - row_delta)).astype(BF16)
            sums[0, place] += jnp.dot(dscores, q, preferred_element_type=F32)
            sums[1, place] += jnp.dot(probs.astype(BF16), o, preferred_element_type=F32)
            dq_ref[...] += lax.dot_general(
                window[0, place], dscores, COLS_BY_COLS, preferred_element_type=F32
            )
            return carry

        lax.fori_loop(0, count, gradients_of, 0)
        dq = jnp.transpose(dq_ref[...] * scale).astype(BF16)
        for g in range(group):
            dqueries_ref[row_ds, g * HEAD_SIZE : (g + 1) * HEAD_SIZE] = dq[
                g * BLOCK_TOKENS : (g + 1) * BLOCK_TOKENS
            ]
        return carry

    above_ref[...] = jnp.zeros_like(above_ref)
    lax.fori_loop(0, own_blocks, one_block, 0)

    @pl.when(jnp.max(above_ref[...]) > ABOVE)
    def _():
        sums[...] = jnp.zeros_like(sums)
        lax.fori_loop(0, own_blocks, careful_block, 0)

    share = tokens // places_out
    for k, out in enumerate(dqueries_refs):
        if head > 0:
            out[:head] = before[k][...]
        first = pl.multiple_of((me_ref[1] ^ k) * share, share)
        out[head] = dqueries_ref[pl.ds(first, share)]
    for j, out in enumerate(outs):
        span = slice(j * tokens, (j + 1) * tokens)
        out[0] = (sums[0, span] * scale).astype(BF16)
        out[1] = sums[1, span].astype(BF16)


def attention(head, cycle_blocks, places_out, scalars, queries, outgrad, window, before):
    tokens = window[OWN].shape[1]
    query_width = queries.shape[0] // tokens * HEAD_SIZE
    rows = query_width // HEAD_SIZE * BLOCK_TOKENS
    part = (2, tokens, HEAD_SIZE)
    shapes = [(head + 1, tokens // places_out, query_width)] * places_out + [part] * SHARDS
    keys_rows = SLOTS * BLOCK_TOKENS
    outs = pl.pallas_call(
        functools.partial(attention_kernel, head, cycle_blocks, places_out),
        out_shape=[jax.ShapeDtypeStruct(shape, BF16) for shape in shapes],
        in_specs=[SMEM] * 3 + [VMEM] * 2 + [ANY] * SHARDS + [VMEM] * len(before),
        out_specs=[VMEM] * len(shapes),
        scratch_shapes=[
            pltpu.VMEM((2, SHARDS * tokens, HEAD_SIZE), BF16),
            pltpu.VMEM((2, SHARDS * tokens, HEAD_SIZE), F32),
            pltpu.VMEM((keys_rows, rows), F32),
            pltpu.VMEM((keys_rows, rows), F32),
            pltpu.VMEM((keys_rows, HEAD_SIZE), BF16),
            pltpu.VMEM((keys_rows, HEAD_SIZE), BF16),
            pltpu.VMEM((tokens, query_width), BF16),
            pltpu.VMEM((8, rows), F32),
            pltpu.VMEM((HEAD_SIZE, rows), F32),
            pltpu.SemaphoreType.DMA((SHARDS,)),
        ],
        compiler_params=pltpu.CompilerParams(vmem_limit_bytes=24 * MIB),
        cost_estimate=pl.CostEstimate(
            flops=10**10, bytes_accessed=2 * 10**7, transcendentals=2 * 10**6
        ),
    )(*scalars, queries, outgrad, *window, *before)
    return outs[:places_out], outs[places_out:]


def arrange_kernel(heads, queries_hbm, outgrad_hbm, *refs):
    outs, sems = refs[: 2 * heads], refs[2 * heads]
    tokens, query_width = queries_hbm.shape
    group = query_width // heads // HEAD_SIZE
    copies = []
    for head in range(heads):
        for i, source in enumerate((queries_hbm, outgrad_hbm)):
            for block in range(tokens // BLOCK_TOKENS):
                for g in range(group):
                    rows = pl.ds(block * BLOCK_TOKENS, BLOCK_TOKENS)
                    columns = pl.ds((head * group + g) * HEAD_SIZE, HEAD_SIZE)
                    to = pl.ds((block * group + g) * BLOCK_TOKENS, BLOCK_TOKENS)
                    copies.append(
                        pltpu.make_async_copy(
                            source.at[rows, columns],
                            outs[2 * head + i].at[to],
                            sems.at[head, i, block, g],
                        )
                    )
    for copy in copies:
        copy.start()
    for copy in copies:
        copy.wait()


def arrange(heads, queries, outgrad):
    tokens, query_width = queries.shape
    group = query_width // heads // HEAD_SIZE
    out = jax.ShapeDtypeStruct((tokens * group, HEAD_SIZE), BF16)
    outs = pl.pallas_call(
        functools.partial(arrange_kernel, heads),
        out_shape=[out] * (2 * heads),
        in_specs=[HBM] * 2,
        out_specs=[VMEM] * (2 * heads),
        scratch_shapes=[pltpu.SemaphoreType.DMA((heads, 2, tokens // BLOCK_TOKENS, group))],
        compiler_params=pltpu.CompilerParams(vmem_limit_bytes=8 * MIB),
        cost_estimate=pl.CostEstimate(flops=0, bytes_accessed=8 * MIB, transcendentals=0),
    )(queries, outgrad)
    return [outs[2 * head : 2 * head + 2] for head in range(heads)]


def pack_kernel(heads, keys_hbm, values_hbm, *refs):
    outs, sems = refs[:heads], refs[heads]
    copies = []
    for head, out in enumerate(outs):
        columns = pl.ds(head * HEAD_SIZE, HEAD_SIZE)
        for i, source in enumerate((keys_hbm, values_hbm)):
            copies.append(
                pltpu.make_async_copy(source.at[:, columns], out.at[i], sems.at[head, i])
            )
    for copy in copies:
        copy.start()
    for copy in copies:
        copy.wait()


def pack(keys, values):
    heads = keys.shape[1] // HEAD_SIZE
    return pl.pallas_call(
        functools.partial(pack_kernel, heads),
        out_shape=[jax.ShapeDtypeStruct((2, keys.shape[0], HEAD_SIZE), BF16)] * heads,
        in_specs=[HBM] * 2,
        out_specs=[VMEM] * heads,
        scratch_shapes=[pltpu.SemaphoreType.DMA((heads, 2))],
        compiler_params=pltpu.CompilerParams(vmem_limit_bytes=56 * MIB),
    )(keys, values)


def sum_kernel(heads, places_out, me_ref, *refs):
    outs = refs[4 * heads :]
    share = outs[0].shape[2]
    for k, out in enumerate(outs):
        rows = pl.ds(pl.multiple_of((me_ref[1] ^ k) * share, share), share)
        for head in range(heads):
            parts = [part[:, rows].astype(F32) for part in refs[4 * head : 4 * head + 4]]
            out[head] = ((parts[0] + parts[1]) + (parts[2] + parts[3])).astype(BF16)


def sum_parts(me, parts, places_out):
    heads = len(parts) // 4
    _, tokens, width = parts[0].shape
    piece = jax.ShapeDtypeStruct((heads, 2, tokens // places_out, width), BF16)
    return pl.pallas_call(
        functools.partial(sum_kernel, heads, places_out),
        out_shape=[piece] * places_out,
        in_specs=[SMEM] + [VMEM] * len(parts),
        out_specs=[VMEM] * places_out,
        compiler_params=pltpu.CompilerParams(vmem_limit_bytes=8 * MIB),
    )(me, *parts)


def assemble_kernel(places_out, n_outs, me_ref, *refs):
    pieces, outs, sems = refs[: -n_outs - 1], refs[-n_outs - 1 : -1], refs[-1]
    per, width = pieces[0].shape[0], pieces[0].shape[-1]
    heads = len(pieces) // places_out * per
    copies = []
    for index, piece in enumerate(pieces):
        for part in range(per):
            head = index // places_out * per + part
            place = (me_ref[1] ^ (index % places_out)) * heads + head
            columns = pl.ds(pl.multiple_of(place * width, width), width)
            for i, out in enumerate(outs):
                source = piece.at[part] if n_outs == 1 else piece.at[part, i]
                copies.append(
                    pltpu.make_async_copy(source, out.at[:, columns], sems.at[i, index, part])
                )
    for copy in copies:
        copy.start()
    for copy in copies:
        copy.wait()


def assemble(me, groups, n_outs):
    places_out = len(groups[0])
    pieces = [piece for group in groups for piece in group]
    per, share, width = pieces[0].shape[0], *pieces[0].shape[-2:]
    out = jax.ShapeDtypeStruct((share, len(pieces) * per * width), BF16)
    return pl.pallas_call(
        functools.partial(assemble_kernel, places_out, n_outs),
        out_shape=[out] * n_outs,
        in_specs=[SMEM] + [VMEM] * len(pieces),
        out_specs=[ANY] * n_outs,
        scratch_shapes=[pltpu.SemaphoreType.DMA((n_outs, len(pieces), per))],
        compiler_params=pltpu.CompilerParams(vmem_limit_bytes=4 * MIB),
    )(me, *pieces)


def swap(x):
    return lax.ppermute(x, "ctx", [(i, i ^ 1) for i in range(lax.axis_size("ctx"))])


def far_place(i, by, size):
    return (i + (by if i % 2 == 0 else -by)) % size


def far(x, by):
    size = lax.axis_size("ctx")
    return lax.ppermute(x, "ctx", [(i, far_place(i, by, size)) for i in range(size)])


def after(x, *others):
    return lax.optimization_barrier((x, *others))[0] if others else x


def exchange(pieces):
    return [
        piece if k == 0 else lax.ppermute(piece, "head", [(i, i ^ k) for i in range(len(pieces))])
        for k, piece in enumerate(pieces)
    ]


def on_device(queries, keys, values, output_gradient, blocks, counts):
    tokens = queries.shape[0]
    cycle_blocks = lax.axis_size("ctx") * (tokens // BLOCK_TOKENS)
    places_out = lax.axis_size("head")
    me = jnp.stack([lax.axis_index("ctx"), lax.axis_index("head")])
    heads = keys.shape[1] // HEAD_SIZE

    rows = arrange(heads, queries, output_gradient)
    windows = []
    for own in pack(keys, values):
        if windows:
            own = after(own, windows[-1][AHEAD])
        ahead, behind, other = far(own, -REACH), far(own, REACH), swap(own)
        crossed = swap(ahead if windows else after(ahead, *rows[0]))
        windows.append([behind, crossed, own, other, ahead])
    dq, parts, sent = [], [], ()
    for head, ((q_rows, o_rows), window) in enumerate(zip(rows, windows)):
        dq, outs = attention(
            head, cycle_blocks, places_out, (blocks, counts, me), q_rows, o_rows, window, dq
        )
        outs = after(outs, *sent)
        last = head == heads - 1
        if last:
            dq = exchange(dq)
        plain, near = far(outs[BEHIND], -REACH), swap(outs[CROSS])
        joined = (outs[AHEAD].astype(F32) + near.astype(F32)).astype(BF16)
        other = swap(after(outs[OTHER], dq[2]) if last else outs[OTHER])
        sent = (near, plain, other)
        parts += [outs[OWN], other, plain, far(joined, REACH)]
    (dqueries,) = assemble(me, [dq], 1)
    dkv_pieces = exchange(sum_parts(me, parts, places_out))
    dkeys, dvalues = assemble(me, [dkv_pieces], 2)
    return dqueries, dkeys, dvalues


def solution(mesh):
    return jax.shard_map(
        on_device,
        mesh=mesh,
        in_specs=(
            P("ctx", "head"),
            P("ctx", "head"),
            P("ctx", "head"),
            P("ctx", "head"),
            P("ctx", None),
            P("ctx"),
        ),
        out_specs=(P(("ctx", "head"), None), P(("ctx", "head"), None), P(("ctx", "head"), None)),
        check_vma=False,
    )
```

```python
import functools
import math

import jax
import jax.numpy as jnp
from jax import lax
from jax.experimental import pallas as pl
from jax.experimental.pallas import tpu as pltpu
from jax.sharding import PartitionSpec as P

HEAD_SIZE = 128
BLOCK_TOKENS = 128
SLOTS = 8
REACH = 2
SHARDS = 2 * REACH + 1
F32 = jnp.float32
BF16 = jnp.bfloat16
ROWS_BY_ROWS = (((1,), (1,)), ((), ()))
COLS_BY_COLS = (((0,), (0,)), ((), ()))
MIB = 2**20
ABOVE = 64.0

VMEM = pl.BlockSpec(memory_space=pltpu.VMEM)
SMEM = pl.BlockSpec(memory_space=pltpu.SMEM)
HBM = pl.BlockSpec(memory_space=pltpu.HBM)
ANY = pl.BlockSpec(memory_space=pl.ANY)

BEHIND, CROSS, OWN, OTHER, AHEAD = range(SHARDS)


def attention_kernel(head, cycle_blocks, places_out, *refs):
    blocks_ref, counts_ref, me_ref, queries, outgrad = refs[:5]
    window_hbm, refs = refs[5 : 5 + SHARDS], refs[5 + SHARDS :]
    if head > 0:
        before, refs = refs[:places_out], refs[places_out:]
    dqueries_refs, refs = refs[:places_out], refs[places_out:]
    outs, refs = refs[:SHARDS], refs[SHARDS:]
    window, sums, scores_ref, dprobs_ref = refs[:4]
    block_keys, block_values, dqueries_ref, above_ref, dq_ref, sems = refs[4:]
    tokens, query_width = dqueries_ref.shape
    group = query_width // HEAD_SIZE
    own_blocks, rows = tokens // BLOCK_TOKENS, group * BLOCK_TOKENS
    scale = 1.0 / math.sqrt(HEAD_SIZE)
    scale_log2 = scale * math.log2(math.e)

    copies = []
    for j in range(SHARDS):
        place = window.at[:, pl.ds(j * tokens, tokens), :]
        copies.append(pltpu.make_async_copy(window_hbm[j], place, sems.at[j]))
    for copy in copies:
        copy.start()
    sums[...] = jnp.zeros_like(sums)
    for copy in copies:
        copy.wait()
    half = cycle_blocks // 2
    me_block = me_ref[0] * own_blocks
    mirrored = me_ref[0] % 2 == 1

    def window_place(qblock, s):
        ahead = lax.rem(blocks_ref[qblock, s] - me_block + half + cycle_blocks, cycle_blocks)
        place = ahead - half + REACH * own_blocks
        shard = lax.div(place, own_blocks)
        flipped = place + (2 * REACH - 2 * shard) * own_blocks
        place = jnp.where(mirrored, flipped, place)
        return pl.ds(pl.multiple_of(place * BLOCK_TOKENS, BLOCK_TOKENS), BLOCK_TOKENS)

    def query_block(qblock, live):
        row_ds = pl.ds(pl.multiple_of(qblock * BLOCK_TOKENS, BLOCK_TOKENS), BLOCK_TOKENS)
        q_cols = [slice(g * HEAD_SIZE, (g + 1) * HEAD_SIZE) for g in range(group)]
        slots = [slice(s * BLOCK_TOKENS, (s + 1) * BLOCK_TOKENS) for s in range(live)]
        places = []
        for s in range(live):
            place = window_place(qblock, s)
            places.append(place)
            block_keys[slots[s]] = window[0, place]
            block_values[slots[s]] = window[1, place]
        q_ds = pl.ds(pl.multiple_of(qblock * rows, rows), rows)
        q, o = queries[q_ds], outgrad[q_ds]

        def fold(x, op):
            return op(x.reshape(BLOCK_TOKENS // 8, 8, rows), axis=0)

        total = weighted = top = None
        for s in range(live):
            scores = lax.dot_general(
                block_keys[slots[s]], q, ROWS_BY_ROWS, preferred_element_type=F32
            )
            top = fold(scores, jnp.max) if s == 0 else jnp.maximum(top, fold(scores, jnp.max))
            if s == 0:
                shift = jnp.max(top, axis=0, keepdims=True) * scale_log2
            dprobs = lax.dot_general(
                block_values[slots[s]], o, ROWS_BY_ROWS, preferred_element_type=F32
            )
            weights = jnp.exp2(scores * scale_log2 - shift)
            dprobs_ref[slots[s]] = dprobs
            scores_ref[slots[s]] = weights
            part, wpart = fold(weights, jnp.sum), fold(weights * dprobs, jnp.sum)
            total = part if s == 0 else total + part
            weighted = wpart if s == 0 else weighted + wpart
        above_ref[...] = jnp.maximum(above_ref[...], top * scale_log2 - shift)
        inverse = 1.0 / jnp.sum(total, axis=0, keepdims=True)
        row_delta = jnp.sum(weighted, axis=0, keepdims=True) * inverse
        dq = None
        for s in range(live):
            probs = scores_ref[slots[s]] * inverse
            dscores = (probs * (dprobs_ref[slots[s]] - row_delta)).astype(BF16)
            sums[0, places[s]] += jnp.dot(dscores, q, preferred_element_type=F32)
            sums[1, places[s]] += jnp.dot(probs.astype(BF16), o, preferred_element_type=F32)
            part = lax.dot_general(
                block_keys[slots[s]], dscores, COLS_BY_COLS, preferred_element_type=F32
            )
            dq = part if s == 0 else dq + part
        dq = jnp.transpose(dq * scale).astype(BF16)
        for g in range(group):
            dqueries_ref[row_ds, q_cols[g]] = dq[g * BLOCK_TOKENS : (g + 1) * BLOCK_TOKENS]

    def one_block(qblock, carry):
        count = counts_ref[qblock]

        def among(least, most):
            if least == most:
                return functools.partial(query_block, qblock, least)
            middle = (least + most) // 2
            return lambda: lax.cond(count <= middle, among(least, middle), among(middle + 1, most))

        among(1, SLOTS)()
        return carry

    def careful_block(qblock, carry):
        row_ds = pl.ds(pl.multiple_of(qblock * BLOCK_TOKENS, BLOCK_TOKENS), BLOCK_TOKENS)
        q_ds = pl.ds(pl.multiple_of(qblock * rows, rows), rows)
        q, o = queries[q_ds], outgrad[q_ds]
        count = counts_ref[qblock]

        def fold(x, op):
            return op(x.reshape(BLOCK_TOKENS // 8, 8, rows), axis=0)

        def slot(s):
            place = window_place(qblock, s)
            return place, pl.ds(pl.multiple_of(s * BLOCK_TOKENS, BLOCK_TOKENS), BLOCK_TOKENS)

        def scores_of(s, top):
            place, to = slot(s)
            scores_ref[to] = lax.dot_general(
                window[0, place], q, ROWS_BY_ROWS, preferred_element_type=F32
            )
            return jnp.maximum(top, fold(scores_ref[to], jnp.max))

        top = lax.fori_loop(0, count, scores_of, jnp.full((8, rows), -jnp.inf, F32))
        row_max = jnp.max(top, axis=0, keepdims=True) * scale_log2

        def weights_of(s, sums_so_far):
            place, to = slot(s)
            dprobs = lax.dot_general(
                window[1, place], o, ROWS_BY_ROWS, preferred_element_type=F32
            )
            weights = jnp.exp2(scores_ref[to] * scale_log2 - row_max)
            dprobs_ref[to] = dprobs
            scores_ref[to] = weights
            total, weighted = sums_so_far
            return total + fold(weights, jnp.sum), weighted + fold(weights * dprobs, jnp.sum)

        zeros = jnp.zeros((8, rows), F32)
        total, weighted = lax.fori_loop(0, count, weights_of, (zeros, zeros))
        inverse = 1.0 / jnp.sum(total, axis=0, keepdims=True)
        row_delta = jnp.sum(weighted, axis=0, keepdims=True) * inverse
        dq_ref[...] = jnp.zeros_like(dq_ref)

        def gradients_of(s, carry):
            place, to = slot(s)
            probs = scores_ref[to] * inverse
            dscores = (probs * (dprobs_ref[to] - row_delta)).astype(BF16)
            sums[0, place] += jnp.dot(dscores, q, preferred_element_type=F32)
            sums[1, place] += jnp.dot(probs.astype(BF16), o, preferred_element_type=F32)
            dq_ref[...] += lax.dot_general(
                window[0, place], dscores, COLS_BY_COLS, preferred_element_type=F32
            )
            return carry

        lax.fori_loop(0, count, gradients_of, 0)
        dq = jnp.transpose(dq_ref[...] * scale).astype(BF16)
        for g in range(group):
            dqueries_ref[row_ds, g * HEAD_SIZE : (g + 1) * HEAD_SIZE] = dq[
                g * BLOCK_TOKENS : (g + 1) * BLOCK_TOKENS
            ]
        return carry

    above_ref[...] = jnp.zeros_like(above_ref)
    lax.fori_loop(0, own_blocks, one_block, 0)

    @pl.when(jnp.max(above_ref[...]) > ABOVE)
    def _():
        sums[...] = jnp.zeros_like(sums)
        lax.fori_loop(0, own_blocks, careful_block, 0)

    share = tokens // places_out
    for k, out in enumerate(dqueries_refs):
        if head > 0:
            out[:head] = before[k][...]
        first = pl.multiple_of((me_ref[1] ^ k) * share, share)
        out[head] = dqueries_ref[pl.ds(first, share)]
    for j, out in enumerate(outs):
        span = slice(j * tokens, (j + 1) * tokens)
        out[0] = (sums[0, span] * scale).astype(BF16)
        out[1] = sums[1, span].astype(BF16)


def attention(head, cycle_blocks, places_out, scalars, queries, outgrad, window, before):
    tokens = window[OWN].shape[1]
    query_width = queries.shape[0] // tokens * HEAD_SIZE
    rows = query_width // HEAD_SIZE * BLOCK_TOKENS
    part = (2, tokens, HEAD_SIZE)
    shapes = [(head + 1, tokens // places_out, query_width)] * places_out + [part] * SHARDS
    keys_rows = SLOTS * BLOCK_TOKENS
    outs = pl.pallas_call(
        functools.partial(attention_kernel, head, cycle_blocks, places_out),
        out_shape=[jax.ShapeDtypeStruct(shape, BF16) for shape in shapes],
        in_specs=[SMEM] * 3 + [VMEM] * 2 + [ANY] * SHARDS + [VMEM] * len(before),
        out_specs=[VMEM] * len(shapes),
        scratch_shapes=[
            pltpu.VMEM((2, SHARDS * tokens, HEAD_SIZE), BF16),
            pltpu.VMEM((2, SHARDS * tokens, HEAD_SIZE), F32),
            pltpu.VMEM((keys_rows, rows), F32),
            pltpu.VMEM((keys_rows, rows), F32),
            pltpu.VMEM((keys_rows, HEAD_SIZE), BF16),
            pltpu.VMEM((keys_rows, HEAD_SIZE), BF16),
            pltpu.VMEM((tokens, query_width), BF16),
            pltpu.VMEM((8, rows), F32),
            pltpu.VMEM((HEAD_SIZE, rows), F32),
            pltpu.SemaphoreType.DMA((SHARDS,)),
        ],
        compiler_params=pltpu.CompilerParams(vmem_limit_bytes=24 * MIB),
        cost_estimate=pl.CostEstimate(
            flops=10**10, bytes_accessed=2 * 10**7, transcendentals=2 * 10**6
        ),
    )(*scalars, queries, outgrad, *window, *before)
    return outs[:places_out], outs[places_out:]


def arrange_kernel(heads, queries_hbm, outgrad_hbm, *refs):
    outs, sems = refs[: 2 * heads], refs[2 * heads]
    tokens, query_width = queries_hbm.shape
    group = query_width // heads // HEAD_SIZE
    copies = []
    for head in range(heads):
        for i, source in enumerate((queries_hbm, outgrad_hbm)):
            for block in range(tokens // BLOCK_TOKENS):
                for g in range(group):
                    rows = pl.ds(block * BLOCK_TOKENS, BLOCK_TOKENS)
                    columns = pl.ds((head * group + g) * HEAD_SIZE, HEAD_SIZE)
                    to = pl.ds((block * group + g) * BLOCK_TOKENS, BLOCK_TOKENS)
                    copies.append(
                        pltpu.make_async_copy(
                            source.at[rows, columns],
                            outs[2 * head + i].at[to],
                            sems.at[head, i, block, g],
                        )
                    )
    for copy in copies:
        copy.start()
    for copy in copies:
        copy.wait()


def arrange(heads, queries, outgrad):
    tokens, query_width = queries.shape
    group = query_width // heads // HEAD_SIZE
    out = jax.ShapeDtypeStruct((tokens * group, HEAD_SIZE), BF16)
    outs = pl.pallas_call(
        functools.partial(arrange_kernel, heads),
        out_shape=[out] * (2 * heads),
        in_specs=[HBM] * 2,
        out_specs=[VMEM] * (2 * heads),
        scratch_shapes=[pltpu.SemaphoreType.DMA((heads, 2, tokens // BLOCK_TOKENS, group))],
        compiler_params=pltpu.CompilerParams(vmem_limit_bytes=8 * MIB),
        cost_estimate=pl.CostEstimate(flops=0, bytes_accessed=8 * MIB, transcendentals=0),
    )(queries, outgrad)
    return [outs[2 * head : 2 * head + 2] for head in range(heads)]


def sum_kernel(heads, places_out, me_ref, *refs):
    outs = refs[4 * heads :]
    share = outs[0].shape[2]
    for k, out in enumerate(outs):
        rows = pl.ds(pl.multiple_of((me_ref[1] ^ k) * share, share), share)
        for head in range(heads):
            parts = [part[:, rows].astype(F32) for part in refs[4 * head : 4 * head + 4]]
            out[head] = ((parts[0] + parts[1]) + (parts[2] + parts[3])).astype(BF16)


def sum_parts(me, parts, places_out):
    heads = len(parts) // 4
    _, tokens, width = parts[0].shape
    piece = jax.ShapeDtypeStruct((heads, 2, tokens // places_out, width), BF16)
    return pl.pallas_call(
        functools.partial(sum_kernel, heads, places_out),
        out_shape=[piece] * places_out,
        in_specs=[SMEM] + [VMEM] * len(parts),
        out_specs=[VMEM] * places_out,
        compiler_params=pltpu.CompilerParams(vmem_limit_bytes=8 * MIB),
    )(me, *parts)


def assemble_kernel(places_out, n_outs, me_ref, *refs):
    pieces, outs, sems = refs[: -n_outs - 1], refs[-n_outs - 1 : -1], refs[-1]
    per, width = pieces[0].shape[0], pieces[0].shape[-1]
    heads = len(pieces) // places_out * per
    copies = []
    for index, piece in enumerate(pieces):
        for part in range(per):
            head = index // places_out * per + part
            place = (me_ref[1] ^ (index % places_out)) * heads + head
            columns = pl.ds(pl.multiple_of(place * width, width), width)
            for i, out in enumerate(outs):
                source = piece.at[part] if n_outs == 1 else piece.at[part, i]
                copies.append(
                    pltpu.make_async_copy(source, out.at[:, columns], sems.at[i, index, part])
                )
    for copy in copies:
        copy.start()
    for copy in copies:
        copy.wait()


def assemble(me, groups, n_outs):
    places_out = len(groups[0])
    pieces = [piece for group in groups for piece in group]
    per, share, width = pieces[0].shape[0], *pieces[0].shape[-2:]
    out = jax.ShapeDtypeStruct((share, len(pieces) * per * width), BF16)
    return pl.pallas_call(
        functools.partial(assemble_kernel, places_out, n_outs),
        out_shape=[out] * n_outs,
        in_specs=[SMEM] + [VMEM] * len(pieces),
        out_specs=[ANY] * n_outs,
        scratch_shapes=[pltpu.SemaphoreType.DMA((n_outs, len(pieces), per))],
        compiler_params=pltpu.CompilerParams(vmem_limit_bytes=4 * MIB),
    )(me, *pieces)


def swap(x):
    return lax.ppermute(x, "ctx", [(i, i ^ 1) for i in range(lax.axis_size("ctx"))])


def far_place(i, by, size):
    return (i + (by if i % 2 == 0 else -by)) % size


def far(x, by):
    size = lax.axis_size("ctx")
    return lax.ppermute(x, "ctx", [(i, far_place(i, by, size)) for i in range(size)])


def after(x, *others):
    return lax.optimization_barrier((x, *others))[0] if others else x


def exchange(pieces):
    return [
        piece if k == 0 else lax.ppermute(piece, "head", [(i, i ^ k) for i in range(len(pieces))])
        for k, piece in enumerate(pieces)
    ]


def on_device(queries, keys, values, output_gradient, blocks, counts):
    tokens = queries.shape[0]
    cycle_blocks = lax.axis_size("ctx") * (tokens // BLOCK_TOKENS)
    places_out = lax.axis_size("head")
    me = jnp.stack([lax.axis_index("ctx"), lax.axis_index("head")])
    heads = keys.shape[1] // HEAD_SIZE

    rows = arrange(heads, queries, output_gradient)
    windows = []
    for head in range(heads):
        columns = slice(head * HEAD_SIZE, (head + 1) * HEAD_SIZE)
        own = jnp.stack([keys[:, columns], values[:, columns]])
        if windows:
            own = after(own, windows[-1][AHEAD])
        ahead, behind, other = far(own, -REACH), far(own, REACH), swap(own)
        crossed = swap(ahead if windows else after(ahead, *rows[0]))
        windows.append([behind, crossed, own, other, ahead])
    dq, parts, sent = [], [], ()
    for head, ((q_rows, o_rows), window) in enumerate(zip(rows, windows)):
        dq, outs = attention(
            head, cycle_blocks, places_out, (blocks, counts, me), q_rows, o_rows, window, dq
        )
        outs = after(outs, *sent)
        last = head == heads - 1
        if last:
            dq = exchange(dq)
        plain, near = far(outs[BEHIND], -REACH), swap(outs[CROSS])
        joined = (outs[AHEAD].astype(F32) + near.astype(F32)).astype(BF16)
        other = swap(after(outs[OTHER], dq[2]) if last else outs[OTHER])
        sent = (near, plain, other)
        parts += [outs[OWN], other, plain, far(joined, REACH)]
    (dqueries,) = assemble(me, [dq], 1)
    dkv_pieces = exchange(sum_parts(me, parts, places_out))
    dkeys, dvalues = assemble(me, [dkv_pieces], 2)
    return dqueries, dkeys, dvalues


def solution(mesh):
    return jax.shard_map(
        on_device,
        mesh=mesh,
        in_specs=(
            P("ctx", "head"),
            P("ctx", "head"),
            P("ctx", "head"),
            P("ctx", "head"),
            P("ctx", None),
            P("ctx"),
        ),
        out_specs=(P(("ctx", "head"), None), P(("ctx", "head"), None), P(("ctx", "head"), None)),
        check_vma=False,
    )
```
